512 devices in a mesh: inst: 32 (over z_lo, y), tp: 16 (over x, z_hi, core).
Axes of the slice: x: 4, y: 4, z: 16 (z_hi: 2, z_lo: 8; z = z_hi * 8 + z_lo), core: 2. Of those that a mesh axis runs over, the one named last changes fastest.
Arguments:
- x_one: bfloat16 [96, 8192], P('inst', 'tp'), may hold values from -6 to 6
- z_one: bfloat16 [96, 8192], P('inst', 'tp'), may hold values from -6 to 6
- dt_one: bfloat16 [96, 128], P('inst', 'tp'), may hold values from -6 to 6
- b_one: bfloat16 [96, 1024], P('inst'), may hold values from -6 to 6
- c_one: bfloat16 [96, 1024], P('inst'), may hold values from -0.625 to 0.625
- q_one: bfloat16 [96, 8192], P('inst')
- kv_one: bfloat16 [96, 2048], P('inst'), may hold values from -6 to 6
- state: float32 [96, 128, 64, 256], P('inst', 'tp'), may hold values from -6 to 6
- cache: bfloat16 [384, 16, 32768], P('inst', None, 'tp'), may hold values from -6 to 6
- page_table: int32 [96, 64], P('inst', 'tp'), may hold values from 0 to 11, as said below
- lengths: int32 [96], replicated, may hold values from 1 to 1022, as said below
- migration: int32 [32, 2], replicated, may hold values from 0 to 95, as said below
- decay_rate: float32 [128], P('tp'), may hold values from 0.02 to 8
- dt_bias: float32 [128], P('tp'), may hold values from -1 to 1
- skip_gain: float32 [128], P('tp'), may hold values from 0.5 to 1.5
- norm_gain: float32 [8192], P('tp'), may hold values from 0.5 to 1.5
- x_two: bfloat16 [96, 8192], P('inst', 'tp'), may hold values from -6 to 6
- z_two: bfloat16 [96, 8192], P('inst', 'tp'), may hold values from -6 to 6
- dt_two: bfloat16 [96, 128], P('inst', 'tp'), may hold values from -6 to 6
- b_two: bfloat16 [96, 1024], P('inst'), may hold values from -6 to 6
- c_two: bfloat16 [96, 1024], P('inst'), may hold values from -0.625 to 0.625
- q_two: bfloat16 [96, 8192], P('inst')
- kv_two: bfloat16 [96, 2048], P('inst'), may hold values from -6 to 6
Outputs:
- mamba_one: bfloat16 [96, 8192], P('inst', 'tp')
- attn_one: bfloat16 [96, 8192], P('inst')
- mamba_two: bfloat16 [96, 8192], P('inst', 'tp')
- attn_two: bfloat16 [96, 8192], P('inst')
- state_out: float32 [96, 128, 64, 256], P('inst', 'tp')
The draws below stay inside these ranges and needn't reach their ends.
Inputs may be any that keep to these rules, and one draw needn't show every extreme that they name: `migration`: column 0 of row i is a request of instance i, between i * 3 and i * 3 + 2; the last instance gives away its last request; column 1 of row i is i XOR m, for one m between 1 and 31 common to all rows. `page_table`: every device's block of 3 x 4 entries is a permutation of its 12 pool pages. `lengths`: some request reaches the largest length.
All inputs are finite; a program needn't handle non-finite values.
Results may differ from the reference program's by a relative error of at most 0.0075.
Values may be sent and summed in bfloat16 or wider, within the bound.
No kernel may reach another device: no remote copies, remote signals or barrier semaphores. Data moves between devices by JAX's collectives and lax.ppermute only.
A program may use at most 64 MiB of HBM per device.

```python
import math
import jax
import jax.numpy as jnp
from jax import lax

MH = 128
HDIM = 64
STATE = 256
HPG = 32
QHEADS = 64
KVHEADS = 8
QDIM = 128
PAGE = 16
PP = 4
REQ = 3
GROUPS = 4
KVW = 2048
POOL = 12
CTX = 1024
R = 96
N_INST = 32
N_TP = 16


def query_rows(key, scale_hi):
    base = jax.random.normal(key, (R, QHEADS, QDIM), jnp.float32)
    scales = jnp.exp(jax.random.uniform(jax.random.fold_in(key, 1), (R, QHEADS, 1), jnp.float32, 0.0, jnp.log(scale_hi)))
    return jnp.clip(base * scales, -200.0, 200.0).reshape(R, QHEADS * QDIM)


def draw_q_one(key, part):
    key = jax.random.fold_in(key, 21)
    return query_rows(key, 1.0).astype(jnp.bfloat16)


def draw_q_two(key, part):
    key = jax.random.fold_in(key, 22)
    return query_rows(key, 1.0).astype(jnp.bfloat16)


def draw_migration(key, part):
    key = jax.random.fold_in(key, 31)
    first, second = jax.random.split(key)
    pairing = jax.random.randint(first, (), 1, N_INST, jnp.int32)
    target = jnp.bitwise_xor(jnp.arange(N_INST, dtype=jnp.int32), pairing).astype(jnp.int32)
    slots = jax.random.randint(second, (N_INST,), 0, REQ, jnp.int32)
    slots = slots.at[N_INST - 1].set(REQ - 1)
    ids = jnp.arange(N_INST, dtype=jnp.int32) * REQ + slots
    return jnp.stack([ids, target], axis=1).astype(jnp.int32)


def draw_page_table(key, part):
    key = jax.random.fold_in(key, 41)
    keys = jax.random.split(key, N_INST * N_TP)
    perms = jax.vmap(lambda k: jax.random.permutation(k, POOL))(keys).astype(jnp.int32)
    perms = perms.reshape(N_INST, N_TP, REQ, PP).transpose(0, 2, 1, 3)
    return perms.reshape(R, N_TP * PP).astype(jnp.int32)


def draw_lengths(key, part):
    key = jax.random.fold_in(key, 51)
    first, second, third = jax.random.split(key, 3)
    vals = jax.random.randint(first, (R,), 1, CTX - 1, jnp.int32)
    top = jax.random.randint(second, (), 0, R, jnp.int32)
    low = jax.random.randint(third, (), 0, R, jnp.int32)
    vals = vals.at[low].set(1)
    return vals.at[top].set(CTX - 2).astype(jnp.int32)


def level_of(key, dims, cuts, smallest, top_value):
    def one(position, blocks):
        steps = jax.random.uniform(jax.random.fold_in(jax.random.fold_in(key, 6), position), (blocks,), jnp.float32, smallest / len(cuts), top_value / len(cuts))
        return jnp.repeat(jnp.exp(steps), dims[position] // blocks).reshape((-1,) + (1,) * (len(dims) - position - 1))

    factor_of = one(*cuts[0])
    for cut in cuts[1:]:
        factor_of = factor_of * one(*cut)
    return factor_of


def scatter_about(key, dims, width, limit, cuts=(), kind=jnp.bfloat16):
    result = jax.random.normal(key, dims, jnp.float32) * width
    if len(cuts) > 0:
        result = level_of(key, dims, cuts, -0.22, 0.18) * result
    return jnp.clip(result, min=-limit, max=limit).astype(kind)


def setup_inputs(seed: int = 0) -> dict:
    arg_keys = jax.random.split(jax.random.key(seed), 24)
    x_one = scatter_about(arg_keys[0], (R, MH * HDIM), 1.0, 6.0, ((0, 32), (1, 16)))
    z_one = scatter_about(arg_keys[1], (R, MH * HDIM), 1.0, 6.0, ((0, 32), (1, 16)))
    dt_one = scatter_about(arg_keys[2], (R, MH), 1.0, 6.0, ((0, 32), (1, 16)))
    b_one = scatter_about(arg_keys[3], (R, GROUPS * STATE), 1.0, 6.0, ((0, 32),))
    c_one = scatter_about(arg_keys[4], (R, GROUPS * STATE), 0.1, 0.625, ((0, 32),))
    q_one = draw_q_one(jax.random.fold_in(arg_keys[23], 71), 0)
    kv_one = scatter_about(arg_keys[6], (R, KVW), 1.0, 6.0, ((0, 32),))
    state = scatter_about(arg_keys[7], (R, MH, HDIM, STATE), 1.0, 6.0, ((0, 32), (1, 16)), jnp.float32)
    cache = scatter_about(arg_keys[8], (N_INST * POOL, PAGE, N_TP * KVW), 1.0, 6.0, ((0, 32), (2, 16)))
    page_table = draw_page_table(jax.random.fold_in(arg_keys[23], 71), 0)
    lengths = draw_lengths(jax.random.fold_in(arg_keys[23], 71), 0)
    migration = draw_migration(jax.random.fold_in(arg_keys[23], 71), 0)
    decay_rate = jnp.clip(jnp.exp(math.log(8.0) - 5.9914646 * jax.random.uniform(arg_keys[12], (MH,), jnp.float32) ** level_of(arg_keys[12], (MH,), ((0, 16),), -0.2, 0.2)), 0.02, 8.0)
    dt_bias = jnp.clip(jax.random.uniform(arg_keys[13], (MH,), jnp.float32, -1.0, 1.0) * level_of(arg_keys[13], (MH,), ((0, 16),), -0.4, 0.0), -1.0, 1.0)
    skip_gain = jnp.clip(0.5 + 1.0 * jax.random.uniform(arg_keys[14], (MH,), jnp.float32) ** level_of(arg_keys[14], (MH,), ((0, 16),), -0.2, 0.2), 0.5, 1.5)
    norm_gain = jnp.clip(1.0 + 0.1 * jax.random.normal(arg_keys[15], (MH * HDIM,), jnp.float32), 0.5, 1.5)
    x_two = scatter_about(arg_keys[16], (R, MH * HDIM), 1.0, 6.0, ((0, 32), (1, 16)))
    z_two = scatter_about(arg_keys[17], (R, MH * HDIM), 1.0, 6.0, ((0, 32), (1, 16)))
    dt_two = scatter_about(arg_keys[18], (R, MH), 1.0, 6.0, ((0, 32), (1, 16)))
    b_two = scatter_about(arg_keys[19], (R, GROUPS * STATE), 1.0, 6.0, ((0, 32),))
    c_two = scatter_about(arg_keys[20], (R, GROUPS * STATE), 0.1, 0.625, ((0, 32),))
    q_two = draw_q_two(jax.random.fold_in(arg_keys[23], 71), 0)
    kv_two = scatter_about(arg_keys[22], (R, KVW), 1.0, 6.0, ((0, 32),))
    return {"x_one": x_one, "z_one": z_one, "dt_one": dt_one, "b_one": b_one, "c_one": c_one, "q_one": q_one, "kv_one": kv_one, "state": state, "cache": cache, "page_table": page_table, "lengths": lengths, "migration": migration, "decay_rate": decay_rate, "dt_bias": dt_bias, "skip_gain": skip_gain, "norm_gain": norm_gain, "x_two": x_two, "z_two": z_two, "dt_two": dt_two, "b_two": b_two, "c_two": c_two, "q_two": q_two, "kv_two": kv_two}


def update_state(state, x, dt_raw, bh, rate, bias):
    dt = jax.nn.softplus(dt_raw.astype(jnp.float32) + bias)
    decay = jnp.exp(-dt * rate)
    xf = x.astype(jnp.float32).reshape(state.shape[:3])
    return decay[:, :, None, None] * state + (dt[:, :, None] * xf)[:, :, :, None] * bh[:, :, None, :]

def read_out(state, x, z, ch, skip):
    xf = x.astype(jnp.float32).reshape(state.shape[:3])
    y = jnp.einsum('nhpk,nhk->nhp', state, ch, precision=lax.Precision.HIGHEST) + skip[None, :, None] * xf
    return y.reshape(state.shape[0], -1) * jax.nn.silu(z.astype(jnp.float32))

def group_norm(gated, gain):
    rows = gated.shape[0]
    grouped = gated.reshape(rows, GROUPS, -1)
    msq = lax.optimization_barrier(jnp.mean(grouped * grouped, axis=-1))
    scaled = grouped * lax.rsqrt(msq + 1e-05)[:, :, None]
    return (scaled.reshape(rows, -1) * gain).astype(jnp.bfloat16)

def per_head(proj):
    return jnp.repeat(proj.astype(jnp.float32).reshape(proj.shape[0], GROUPS, STATE), HPG, axis=1)

def build_context(cache, page_table, request):
    inst = request // REQ
    table = page_table[request].reshape(N_TP, PP)
    pool = lax.dynamic_slice_in_dim(cache, (inst * POOL).astype(jnp.int32), POOL, 0)
    pool = pool.reshape(POOL, PAGE, N_TP, KVW)
    rows = pool[table, :, jnp.arange(N_TP)[:, None], :]
    return rows.reshape(CTX, KVW)

def put_row(ctx, row, pos):
    hit = jnp.arange(CTX) == pos
    return jnp.where(hit[:, None], row[None, :], ctx)

def attend(query, ctx, upto):
    half = KVHEADS * QDIM
    keys = ctx[:, :half].astype(jnp.float32).reshape(CTX, KVHEADS, QDIM)
    vals = ctx[:, half:].astype(jnp.float32).reshape(CTX, KVHEADS, QDIM)
    qf = query.astype(jnp.float32).reshape(KVHEADS, QHEADS // KVHEADS, QDIM)
    scores = jnp.einsum('gqd,cgd->gqc', qf, keys, precision=lax.Precision.HIGHEST) / jnp.sqrt(jnp.float32(QDIM))
    valid = jnp.arange(CTX) <= upto
    scores = jnp.where(valid[None, None, :], scores, -1e+30)
    top = lax.optimization_barrier(jnp.max(scores, axis=-1, keepdims=True))
    weights = jnp.where(valid[None, None, :], jnp.exp(scores - top), 0.0)
    total = lax.optimization_barrier(jnp.sum(weights, axis=-1, keepdims=True))
    out = jnp.einsum('gqc,cgd->gqd', weights, vals, precision=lax.Precision.HIGHEST) / total
    return out.reshape(-1).astype(jnp.bfloat16)

def reference(x_one, z_one, dt_one, b_one, c_one, q_one, kv_one, state, cache, page_table, lengths, migration, decay_rate, dt_bias, skip_gain, norm_gain, x_two, z_two, dt_two, b_two, c_two, q_two, kv_two):
    state1 = update_state(state, x_one, dt_one, per_head(b_one), decay_rate, dt_bias)
    mamba_one = group_norm(read_out(state1, x_one, z_one, per_head(c_one), skip_gain), norm_gain)

    def first(item):
        request, query, row = item
        ctx = put_row(build_context(cache, page_table, request), row, lengths[request])
        return attend(query, ctx, lengths[request])
    attn_one = lax.map(first, (jnp.arange(R, dtype=jnp.int32), q_one, kv_one))
    anchor = jnp.arange(R, dtype=jnp.int32).at[migration[migration[:, 1], 0]].set(migration[:, 0])
    state_out = update_state(state1[anchor], x_two, dt_two, per_head(b_two), decay_rate, dt_bias)
    mamba_two = group_norm(read_out(state_out, x_two, z_two, per_head(c_two), skip_gain), norm_gain)

    def second(item):
        source, query, row = item
        ctx = put_row(build_context(cache, page_table, source), kv_one[source], lengths[source])
        ctx = put_row(ctx, row, lengths[source] + 1)
        return attend(query, ctx, lengths[source] + 1)
    attn_two = lax.map(second, (anchor, q_two, kv_two))
    return (mamba_one, attn_one, mamba_two, attn_two, state_out)
```

```python
import functools

import jax
import jax.numpy as jnp
from jax import lax
from jax.experimental import pallas as pl
from jax.experimental.pallas import tpu as pltpu
from jax.sharding import PartitionSpec as P

F32 = jnp.float32
BF16 = jnp.bfloat16

HPG = 32
QDIM = 128
STATE = 256
REQ = 3
HEADS = 8
HDIM = 64
COLS = HEADS * HDIM
KVHEADS = 8
QPK = 8
PAGE = 16
POOL = 12
PP = 4
KEYS = POOL * PAGE
EXTRA = 16
NORM = HPG * HDIM
NEG = -1e30

QH, KH = 4096, 1024
AUX = QH + KH
WIDE = AUX + 1536

VMEM = pltpu.VMEM
SMEM = pltpu.SMEM


def iota(shape, dim):
    return lax.broadcasted_iota(jnp.int32, shape, dim)


def split3(v):
    a = v.astype(BF16).astype(F32)
    rest = v - a
    b = rest.astype(BF16).astype(F32)
    c = (rest - b).astype(BF16).astype(F32)
    return a, b, c


def slot_of(mig):
    inst = lax.axis_index("inst")
    return mig[inst, 0] - inst * REQ


def call(body, out_shape, in_specs, out_specs, scratch=(), **kw):
    return pl.pallas_call(
        body,
        out_shape=out_shape,
        in_specs=in_specs,
        out_specs=out_specs,
        scratch_shapes=list(scratch),
        compiler_params=pltpu.CompilerParams(vmem_limit_bytes=40 * 2**20),
        **kw,
    )


def vm(n):
    return [pl.BlockSpec(memory_space=VMEM)] * n


def sm(n):
    return [pl.BlockSpec(memory_space=SMEM)] * n


def expand(per_head, rows):
    head = iota((rows, COLS), 1) // HDIM
    out = jnp.zeros((rows, COLS), F32)
    for h in range(HEADS):
        out = jnp.where(head == h, per_head[:, h : h + 1], out)
    return out


def softplus(v):
    return jnp.maximum(v, 0.0) + jnp.log1p(jnp.exp(-jnp.abs(v)))


def group_cols():
    g = lax.axis_index("tp") * HEADS // HPG
    return pl.ds(pl.multiple_of(g * STATE, STATE), STATE)


def prepare_body(mig, x1, dt1, b1, q2, kv2, x2, z2, dt2, b2, c2, state, out, moving, rows, held, sem):
    slot = slot_of(mig)
    copy = pltpu.make_async_copy(state.at[slot], held, sem)
    copy.start()

    def pick(v):
        v = v.astype(F32)
        return jnp.sum(jnp.where(iota(v.shape, 0) == slot, v, 0.0), axis=0, keepdims=True)

    cols = group_cols()
    rows[...] = jnp.zeros_like(rows)
    q = pick(q2[...])
    kv = pick(kv2[...])
    for k in range(2):
        rows[k : k + 1, :QH] = q[:, k * QH : (k + 1) * QH]
        rows[k : k + 1, QH:AUX] = kv[:, k * KH : (k + 1) * KH]
    rows[0:1, AUX : AUX + 512] = pick(x2[...])
    rows[0:1, AUX + 512 : AUX + 1024] = pick(z2[...])
    rows[0:1, AUX + 1024 : AUX + 1280] = pick(b2[:, cols])
    rows[0:1, AUX + 1280 : AUX + 1536] = pick(c2[:, cols])
    rows[1:2, AUX : AUX + 512] = pick(x1[...])
    rows[1:2, AUX + 512 : AUX + 768] = pick(b1[:, cols])
    rows[1:2, AUX + 768 : AUX + 776] = pick(dt2[...])
    rows[1:2, AUX + 896 : AUX + 904] = pick(dt1[...])
    out[...] = rows[...].astype(BF16)
    copy.wait()
    moving[...] = held[...].astype(BF16)


def prepare(mig, x1, dt1, b1, q2, kv2, x2, z2, dt2, b2, c2, state):
    return call(
        prepare_body,
        (
            jax.ShapeDtypeStruct((2, WIDE), BF16),
            jax.ShapeDtypeStruct(state.shape[1:], BF16),
        ),
        sm(1) + vm(10) + [pl.BlockSpec(memory_space=pl.ANY)],
        tuple(vm(2)),
        [VMEM((2, WIDE), F32), VMEM(state.shape[1:], F32), pltpu.SemaphoreType.DMA],
        name="prepare",
    )(mig, x1, dt1, b1, q2, kv2, x2, z2, dt2, b2, c2, state)


def stats_row(col, sub, lane):
    a, b, c = split3(jnp.broadcast_to(col, col.shape[:2] + (128,)))
    row = jnp.where(
        lane == sub,
        a,
        jnp.where(lane == sub + 8, b, jnp.where(lane == sub + 16, c, 0.0)),
    )
    return jnp.sum(row, axis=1, keepdims=True)


def stats_col(row, sub, lane):
    spread = jnp.broadcast_to(row, (row.shape[0], 8, 128))
    mine = jnp.logical_and(lane < 24, lane % 8 == sub)
    return jnp.sum(jnp.where(mine, spread, 0.0), axis=2, keepdims=True)


def partial_body(
    mig, lens, table, swapped, x1, z1, dt1, b1, c1, q1, kv1, state, cache,
    rate, bias, skip, x2, z2, dt2, b2, c2, q2, kv2,
    blocks, gated, q8, kv16, x8, z8, d8, b8, c8,
):
    slot = slot_of(mig)
    inst = lax.axis_index("inst")
    tp = lax.axis_index("tp")
    cols = group_cols()
    sw = swapped[...].astype(F32)

    def rows8(scr, one, two, moved):
        n = one.shape[-1]
        scr[...] = jnp.zeros_like(scr)
        scr[0:3, :n] = one.astype(F32)
        scr[3:6, :n] = jnp.where(iota((3, n), 0) == slot, moved, two.astype(F32))
        return scr[...]

    q8[6:8, :] = jnp.zeros_like(q8[6:8, :])
    q8[0:3, :] = q1[...].astype(F32)
    q8[3:6, :] = q2[...].astype(F32)
    for k in range(2):
        here = pl.ds(k * QH, QH)
        q8[3:6, here] = jnp.where(iota((3, QH), 0) == slot, sw[k : k + 1, :QH], q8[3:6, here])
    kv16[...] = jnp.zeros_like(kv16)
    kv16[0:3, :] = kv1[...].astype(F32)
    for k in range(2):
        here = pl.ds(k * KH, KH)
        kv16[3:6, here] = jnp.where(
            iota((3, KH), 0) == slot, sw[k : k + 1, QH:AUX], kv2[:, here].astype(F32)
        )

    xx = rows8(x8, x1[...], x2[...], sw[0:1, AUX : AUX + 512])
    zz = rows8(z8, z1[...], z2[...], sw[0:1, AUX + 512 : AUX + 1024])
    bb = rows8(b8, b1[:, cols], b2[:, cols], sw[0:1, AUX + 1024 : AUX + 1280])
    cc = rows8(c8, c1[:, cols], c2[:, cols], sw[0:1, AUX + 1280 : AUX + 1536])
    dd = rows8(d8, dt1[...], dt2[...], sw[1:2, AUX + 768 : AUX + 776])
    dt = softplus(expand(dd, 8) + expand(bias[...], 1))
    decay = jnp.exp(-dt * expand(rate[...], 1))
    read = jnp.zeros((8, COLS), F32)
    row256 = iota((8, STATE), 0)
    for r in range(REQ):
        ch = jnp.where(jnp.logical_or(row256 == r, row256 == r + 3), cc, 0.0).astype(BF16)
        s = state[r].reshape(COLS, STATE)
        hi = s.astype(BF16)
        lo = (s - hi.astype(F32)).astype(BF16)
        for part in (hi, lo):
            read += lax.dot_general(ch, part, (((1,), (1,)), ((), ())), preferred_element_type=F32)
    pushed = dt * xx
    same = jnp.sum(bb * cc, axis=1, keepdims=True)
    cross = jnp.sum(pltpu.roll(bb, 3, 0) * cc, axis=1, keepdims=True)
    first = pltpu.roll(decay, 3, 0) * read + pltpu.roll(pushed, 3, 0) * cross
    second = iota((8, COLS), 0) >= 3
    y = decay * jnp.where(second, first, read) + pushed * same + expand(skip[...], 1) * xx
    g = y * (zz / (1.0 + jnp.exp(-zz)))
    gated[...] = g
    squares = jnp.sum(g * g, axis=1, keepdims=True)

    lane = iota((1, KEYS + EXTRA), 1)
    owner = jnp.full(lane.shape, -1, jnp.int32)
    ok = jnp.zeros(lane.shape, jnp.int32)
    late = jnp.logical_and(lane >= KEYS + REQ, lane < KEYS + 2 * REQ)
    span = PP * PAGE
    for r in range(REQ):
        length = lens[inst * REQ + r]
        for p in range(PP):
            here = (lane // PAGE) == table[r, p]
            pos = tp * span + p * PAGE + lane % PAGE
            owner = jnp.where(here, r, owner)
            ok = jnp.where(jnp.logical_and(here, pos < length), 1, ok)
        for e, at in ((r, length), (r + REQ, length + 1)):
            here = lane == KEYS + e
            owner = jnp.where(here, r, owner)
            ok = jnp.where(jnp.logical_and(here, at // span == tp), 1, ok)
    row = iota((8, KEYS + EXTRA), 0)
    mine = jnp.where(row < 3, row, jnp.where(row < 6, row - 3, -2))
    valid = (mine == owner) & (ok == 1) & ((row >= 3) | jnp.logical_not(late))
    valid = valid.astype(F32)[None]
    sub = iota((QPK, 8, 128), 1)
    lane3 = iota((QPK, 8, 128), 2)
    sq_row = stats_row(jnp.broadcast_to(squares[None], (1, 8, 1)), sub[:1], lane3[:1])
    extra = kv16[...].astype(BF16)
    for k in range(KVHEADS):
        qk = jnp.concatenate(
            [q8[:, (k * QPK + h) * QDIM : (k * QPK + h + 1) * QDIM] for h in range(QPK)], axis=0
        ).astype(BF16)
        kcols = slice(k * QDIM, (k + 1) * QDIM)
        vcols = slice((KVHEADS + k) * QDIM, (KVHEADS + k + 1) * QDIM)
        keys = jnp.concatenate([cache[:, :, kcols].reshape(KEYS, QDIM), extra[:, kcols]], axis=0)
        vals = jnp.concatenate([cache[:, :, vcols].reshape(KEYS, QDIM), extra[:, vcols]], axis=0)
        s = lax.dot_general(qk, keys, (((1,), (1,)), ((), ())), preferred_element_type=F32)
        s = (s * (1.0 / QDIM**0.5)).reshape(QPK, 8, KEYS + EXTRA)
        s = jnp.where(valid > 0.0, s, NEG)
        top = jnp.max(s, axis=2, keepdims=True)
        w = jnp.where(valid > 0.0, jnp.exp(s - top), 0.0).astype(BF16)
        total = jnp.sum(w.astype(F32), axis=2, keepdims=True)
        acc = jnp.dot(
            w.reshape(QPK * 8, KEYS + EXTRA), vals, preferred_element_type=F32
        ).reshape(QPK, 8, QDIM)
        some = total > 0.0
        safe = jnp.where(some, total, 1.0)
        lse = jnp.where(some, top + jnp.log(safe), NEG)
        o = acc / safe
        o = jnp.where(sub == 6, stats_row(lse, sub, lane3), jnp.where(sub == 7, sq_row, o))
        blocks[k] = o.reshape(QPK * 8, QDIM).astype(BF16)


def partials(mig, lens, table, swapped, *rest):
    return call(
        partial_body,
        (
            jax.ShapeDtypeStruct((KVHEADS, QPK * 8, QDIM), BF16),
            jax.ShapeDtypeStruct((8, COLS), F32),
        ),
        sm(3) + vm(1 + len(rest)),
        tuple(vm(2)),
        [
            VMEM((8, KVHEADS * QPK * QDIM), F32),
            VMEM((EXTRA, 2 * KVHEADS * QDIM), F32),
            VMEM((8, COLS), F32),
            VMEM((8, COLS), F32),
            VMEM((8, 128), F32),
            VMEM((8, STATE), F32),
            VMEM((8, STATE), F32),
        ],
        name="partials",
    )(mig, lens, table, swapped, *rest)


def combine_body(mig, recv, gated, mine, moved, scr):
    slot = slot_of(mig)
    x = lax.axis_index("tp") // 4
    sub = iota((QPK, 8, 128), 1)
    lane = iota((QPK, 8, 128), 2)
    lses = []
    for j in range(8):
        rows = recv[j].astype(F32).reshape(QPK, 8, 128)
        lses.append(stats_col(rows[:, 6:7, :], sub, lane))
    top = functools.reduce(jnp.maximum, lses)
    total = jnp.zeros_like(top)
    acc = jnp.zeros((QPK, 8, 128), F32)
    for j in range(8):
        w = jnp.exp(lses[j] - top)
        total += w
        acc += w * recv[j].astype(F32).reshape(QPK, 8, 128)
    o = acc / total
    lse = top + jnp.log(total)
    pair = recv[2 * x].astype(F32)[7:8] + recv[2 * x + 1].astype(F32)[7:8]
    squares = stats_col(pair[None], sub[:1], lane[:1])
    sq_row = stats_row(squares, sub[:1], lane[:1])
    block = jnp.where(sub == 6, stats_row(lse, sub, lane), jnp.where(sub == 7, sq_row, o))
    mine[...] = block.reshape(QPK * 8, 128).astype(BF16)

    here = sub == slot + 3
    lane2 = iota((QPK, 128), 1)

    def terms(v):
        a, b, c = split3(v)
        return jnp.where(lane2 == 0, a, jnp.where(lane2 == 1, b, jnp.where(lane2 == 2, c, 0.0)))

    scr[0:8, :] = jnp.sum(jnp.where(here, o, 0.0), axis=1)
    scr[8:16, :] = terms(jnp.sum(jnp.where(here, lse, 0.0), axis=1))
    g = gated[...]
    g = jnp.sum(jnp.where(iota(g.shape, 0) == slot + 3, g, 0.0), axis=0, keepdims=True)
    hi = g.astype(BF16).astype(F32)
    for k in range(4):
        piece = slice(k * 128, (k + 1) * 128)
        scr[16 + k : 17 + k, :] = hi[:, piece]
        scr[20 + k : 21 + k, :] = (g - hi)[:, piece]
    sq = jnp.sum(jnp.where(here[:1], squares, 0.0), axis=1)
    scr[24:32, :] = terms(jnp.broadcast_to(sq, (8, 128)))
    moved[...] = scr[...].astype(BF16)


def combine(mig, recv, gated):
    return call(
        combine_body,
        (jax.ShapeDtypeStruct((QPK * 8, 128), BF16), jax.ShapeDtypeStruct((32, 128), BF16)),
        sm(1) + vm(2),
        tuple(vm(2)),
        [VMEM((32, 128), F32)],
        name="combine",
    )(mig, recv, gated)


def finish_body(mig, mine, across, near, far, gated, gain, blocks, m1, m2, scr):
    slot = slot_of(mig)
    upper = (lax.axis_index("tp") // 2) % 2 == 1
    sub = iota((QPK, 8, 128), 1)
    lane = iota((QPK, 8, 128), 2)
    own = mine[...].astype(F32).reshape(QPK, 8, 128)
    other = across[...].astype(F32).reshape(QPK, 8, 128)
    same = near[...].astype(F32)
    flip = far[...].astype(F32)

    def merge(a, b, la, lb):
        top = jnp.maximum(la, lb)
        wa = jnp.exp(la - top)
        wb = jnp.exp(lb - top)
        return (wa * a + wb * b) / (wa + wb)

    a = jnp.where(upper, other, own)
    b = jnp.where(upper, own, other)
    o = merge(a, b, stats_col(a[:, 6:7], sub, lane), stats_col(b[:, 6:7], sub, lane))
    sq = stats_col(own[:1, 7:8], sub[:1], lane[:1]) + stats_col(other[:1, 7:8], sub[:1], lane[:1])

    a = jnp.where(upper, flip, same)
    b = jnp.where(upper, same, flip)
    la = jnp.sum(a[8:16], axis=1, keepdims=True)
    lb = jnp.sum(b[8:16], axis=1, keepdims=True)
    om = merge(a[0:8], b[0:8], la, lb)
    o = jnp.where(sub == slot + 3, om[:, None, :], o)
    o = o.reshape(QPK * 8, 128).astype(BF16)
    for k in range(8):
        blocks[k] = o

    sqm = jnp.sum(same[24:25] + flip[24:25], axis=1, keepdims=True)
    gm = same[16:20] + same[20:24]
    scr[...] = gated[...]
    row = iota((8, COLS), 0) == slot + 3
    g = jnp.where(row, jnp.concatenate([gm[k : k + 1] for k in range(4)], axis=1), scr[...])
    total = jnp.where(row, sqm, sq[0])
    scr[...] = g * lax.rsqrt(total * (1.0 / NORM) + 1e-05) * gain[...]
    m1[...] = scr[0:3, :].astype(BF16)
    m2[...] = scr[3:6, :].astype(BF16)


def finish(mig, mine, across, near, far, gated, gain):
    return call(
        finish_body,
        (
            jax.ShapeDtypeStruct((8, QPK * 8, 128), BF16),
            jax.ShapeDtypeStruct((REQ, COLS), BF16),
            jax.ShapeDtypeStruct((REQ, COLS), BF16),
        ),
        sm(1) + vm(6),
        tuple(vm(3)),
        [VMEM((8, COLS), F32)],
        name="finish",
    )(mig, mine, across, near, far, gated, gain)


def spread_body(recv, a1, a2, scr):
    for k in range(KVHEADS):
        rows = recv[k].astype(F32)
        for h in range(QPK):
            at = (k * QPK + h) * QDIM
            scr[:, at : at + QDIM] = rows[h * 8 : (h + 1) * 8]
    a1[...] = scr[0:3, :].astype(BF16)
    a2[...] = scr[3:6, :].astype(BF16)


def spread(recv):
    n = KVHEADS * QPK * QDIM
    return call(
        spread_body,
        (jax.ShapeDtypeStruct((REQ, n), BF16),) * 2,
        vm(1),
        tuple(vm(2)),
        [VMEM((8, n), F32)],
        name="spread",
    )(recv)


def update_body(mig, swapped, arrived, x1, dt1, b1, rate, bias, x2, dt2, b2, state, out, x8, d8, b8):
    slot = slot_of(mig)
    r = pl.program_id(0)
    cols = group_cols()
    sw = swapped[...].astype(F32)

    def rows8(scr, one, two, moved):
        n = one.shape[-1]
        scr[...] = jnp.zeros_like(scr)
        scr[0:3, :n] = jnp.where(iota((3, n), 0) == slot, moved, one.astype(F32))
        scr[3:6, :n] = two.astype(F32)
        return scr[...]

    xx = rows8(x8, x1[...], x2[...], sw[1:2, AUX : AUX + 512])
    bb = rows8(b8, b1[:, cols], b2[:, cols], sw[1:2, AUX + 512 : AUX + 768])
    dd = rows8(d8, dt1[...], dt2[...], sw[1:2, AUX + 896 : AUX + 904])
    dt = softplus(expand(dd, 8) + expand(bias[...], 1))
    decay = jnp.exp(-dt * expand(rate[...], 1))
    pushed = dt * xx
    later = pltpu.roll(decay, 5, 0)
    row = iota((8, COLS), 0)
    u = jnp.where(row < 3, pushed * later, pushed)
    both = jnp.sum(jnp.where(row == r, decay * later, 0.0), axis=0, keepdims=True)
    mine = jnp.logical_or(row == r, row == r + 3)
    u = jnp.where(mine, u, 0.0)
    hi = u.astype(BF16)
    lo = (u - hi.astype(F32)).astype(BF16)
    bh = bb.astype(BF16)
    add = jnp.zeros((COLS, STATE), F32)
    for part in (hi, lo):
        add += lax.dot_general(part, bh, (((0,), (0,)), ((), ())), preferred_element_type=F32)
    moved = r == slot
    for h in range(HEADS):
        s = jnp.where(moved, arrived[h].astype(F32), state[0, h])
        d = both[:, h * HDIM : h * HDIM + 1]
        out[0, h] = d * s + add[h * HDIM : (h + 1) * HDIM]


def update(mig, swapped, arrived, x1, dt1, b1, rate, bias, x2, dt2, b2, state):
    block = pl.BlockSpec((1,) + state.shape[1:], lambda r: (r, 0, 0, 0))
    return call(
        update_body,
        jax.ShapeDtypeStruct(state.shape, F32),
        sm(1) + vm(10) + [block],
        block,
        [VMEM((8, COLS), F32), VMEM((8, 128), F32), VMEM((8, STATE), F32)],
        grid=(REQ,),
        name="update",
    )(mig, swapped, arrived, x1, dt1, b1, rate, bias, x2, dt2, b2, state)


PLANE = [[x * 4 + z * 2 + c for x in range(4) for c in range(2)] for z in range(2)]


def plane_exchange(blocks):
    return lax.all_to_all(blocks, "tp", 0, 0, axis_index_groups=PLANE)


def swap_by(m, flip):
    n_tp = lax.axis_size("tp")
    n = lax.axis_size("inst") * n_tp
    return [(s, s ^ (m * n_tp + flip)) for s in range(n)]


def swap_inputs(m, payload):
    return lax.ppermute(payload, ("inst", "tp"), swap_by(m, 0))


def swap_results(m, moving, mine, moved):
    arrived = lax.ppermute(moving, ("inst", "tp"), swap_by(m, 0))
    across = lax.ppermute(mine, ("inst", "tp"), swap_by(0, 2))
    far = lax.ppermute(moved, ("inst", "tp"), swap_by(m, 2))
    near = lax.ppermute(moved, ("inst", "tp"), swap_by(m, 0))
    return arrived, across, near, far


def shards(
    x_one, z_one, dt_one, b_one, c_one, q_one, kv_one, state, cache, page_table,
    lengths, migration, decay_rate, dt_bias, skip_gain, norm_gain,
    x_two, z_two, dt_two, b_two, c_two, q_two, kv_two,
):
    n_inst = lax.axis_size("inst")
    rate = decay_rate[None]
    bias = dt_bias[None]
    which = migration[0, 1] - 1
    ways = range(1, n_inst)
    payload, moving = prepare(
        migration, x_one, dt_one, b_one, q_two, kv_two, x_two, z_two, dt_two, b_two, c_two, state
    )
    swapped = lax.switch(which, [functools.partial(swap_inputs, m) for m in ways], payload)
    blocks, gated = partials(
        migration, lengths, page_table, swapped,
        x_one, z_one, dt_one, b_one, c_one, q_one, kv_one, state, cache,
        rate, bias, skip_gain[None], x_two, z_two, dt_two, b_two, c_two, q_two, kv_two,
    )
    mine, moved = combine(migration, plane_exchange(blocks), gated)
    arrived, across, near, far = lax.switch(
        which, [functools.partial(swap_results, m) for m in ways], moving, mine, moved
    )
    blocks, mamba_one, mamba_two = finish(
        migration, mine, across, near, far, gated, norm_gain[None]
    )
    attn_one, attn_two = spread(plane_exchange(blocks))
    state_out = update(
        migration, swapped, arrived, x_one, dt_one, b_one, rate, bias, x_two, dt_two, b_two, state
    )
    return (mamba_one, attn_one, mamba_two, attn_two, state_out)


def solution(mesh):
    row = P("inst", "tp")
    wide = P("inst", None)
    head = P("tp")
    states = P("inst", "tp", None, None)
    return jax.shard_map(
        shards,
        mesh=mesh,
        in_specs=(
            row, row, row, wide, wide, wide, wide, states, P("inst", None, "tp"), row,
            P(), P(), head, head, head, head, row, row, row, wide, wide, wide, wide,
        ),
        out_specs=(row, wide, row, wide, states),
        check_vma=False,
    )
```

```python
import functools

import jax
import jax.numpy as jnp
from jax import lax
from jax.experimental import pallas as pl
from jax.experimental.pallas import tpu as pltpu
from jax.sharding import PartitionSpec as P

F32 = jnp.float32
BF16 = jnp.bfloat16
I32 = jnp.int32

HPG = 32
QDIM = 128
STATE = 256
REQ = 3
HEADS = 8
HALF = HEADS // 2
HDIM = 64
COLS = HEADS * HDIM
STATE_ROWS = HALF * HDIM * 2
KVHEADS = 8
QPK = 8
QHEADS = KVHEADS * QPK
KVW = 2 * KVHEADS * QDIM
PAGE = 16
POOL = 12
PP = 4
SPAN = PP * PAGE
KEYS = POOL * PAGE
EXTRA = 16
NORM = HPG * HDIM
NEG = -1e30
SCALE = 1.0 / QDIM**0.5

KV = QHEADS
X2 = KV + 16
Z2 = X2 + 4
B2 = Z2 + 4
C2 = B2 + 2
D2 = C2 + 2
D1 = D2 + 1
X1 = D1 + 1
B1 = X1 + 4
SWAP = 112

LSE = QHEADS
GHI = LSE + 8
GLO = GHI + 4
MOVED = 80

VMEM = pltpu.VMEM
NT = (((1,), (1,)), ((), ()))


def iota(shape, dim):
    return lax.broadcasted_iota(I32, shape, dim)


def split3(v):
    a = v.astype(BF16).astype(F32)
    rest = v - a
    b = rest.astype(BF16).astype(F32)
    c = (rest - b).astype(BF16).astype(F32)
    return a, b, c


def store_states(out, at, v):
    n = HALF * HDIM
    v = v.reshape(n, STATE).astype(BF16)
    out[at : at + n, :] = v[:, :128]
    out[at + n : at + 2 * n, :] = v[:, 128:]


def load_state(ref, at, h):
    first = at + h * HDIM
    second = first + HALF * HDIM
    return jnp.concatenate([ref[first : first + HDIM, :], ref[second : second + HDIM, :]], axis=1)


def slot_of(mig):
    inst = lax.axis_index("inst")
    return mig[inst, 0] - inst * REQ


def whole(a):
    return pl.BlockSpec(a.shape, lambda i: (0,) * a.ndim)


def here(n):
    return [pl.BlockSpec(memory_space=VMEM)] * n


def scalars(n):
    return [pl.BlockSpec(memory_space=pltpu.SMEM)] * n


def call(body, out_shape, in_specs, out_specs, scratch=(), grid=(1,), **kw):
    return pl.pallas_call(
        body,
        out_shape=out_shape,
        in_specs=in_specs,
        out_specs=out_specs,
        scratch_shapes=list(scratch),
        compiler_params=pltpu.CompilerParams(vmem_limit_bytes=60 * 2**20),
        grid=grid,
        **kw,
    )


def like(*shape, dtype=BF16):
    return jax.ShapeDtypeStruct(shape, dtype)


def expand(per_head, rows):
    head = iota((rows, COLS), 1) // HDIM
    out = jnp.zeros((rows, COLS), F32)
    for h in range(HEADS):
        out = jnp.where(head == h, per_head[:, h : h + 1], out)
    return out


def flat(rows):
    return jnp.concatenate([rows[k : k + 1] for k in range(rows.shape[0])], axis=1)


def softplus(v):
    return jnp.maximum(v, 0.0) + jnp.log1p(jnp.exp(-jnp.abs(v)))


def silu(v):
    return v / (1.0 + jnp.exp(-v))


def group_cols():
    g = lax.axis_index("tp") * HEADS // HPG
    return pl.ds(pl.multiple_of(g * STATE, STATE), STATE)


def hi_lo(v):
    hi = v.astype(BF16)
    return hi, (v - hi.astype(F32)).astype(BF16)


def prepare_body(mig, x1, dt1, b1, q2, kv2, x2, z2, dt2, b2, c2, state, out, rows, held, sem):
    slot = slot_of(mig)
    copy = pltpu.make_async_copy(state.at[slot, :HALF], held, sem)
    copy.start()

    def put(at, v):
        v = v.astype(F32)
        v = jnp.sum(jnp.where(iota(v.shape, 0) == slot, v, 0.0), axis=0, keepdims=True)
        width = min(v.shape[1], 128)
        for k in range(v.shape[1] // width):
            rows[at + k : at + k + 1, :width] = v[:, k * width : (k + 1) * width]

    cols = group_cols()
    rows[D2:, :] = jnp.zeros_like(rows[D2:, :])
    put(0, q2[...])
    put(KV, kv2[...])
    put(X2, x2[...])
    put(Z2, z2[...])
    put(B2, b2[:, cols])
    put(C2, c2[:, cols])
    put(D2, dt2[...])
    put(D1, dt1[...])
    put(X1, x1[...])
    put(B1, b1[:, cols])
    out[:SWAP, :] = rows[...].astype(BF16)
    copy.wait()
    store_states(out, SWAP, held[...])


def prepare(mig, *rest):
    return call(
        prepare_body,
        like(SWAP + STATE_ROWS, 128),
        scalars(1) + [whole(a) for a in rest[:-1]] + [pl.BlockSpec(memory_space=pl.ANY)],
        here(1)[0],
        [VMEM((SWAP, 128), F32), VMEM((HALF, HDIM, STATE), F32), pltpu.SemaphoreType.DMA],
        name="prepare",
    )(mig, *rest)


def stats_row(col, sub, lane):
    a, b, c = split3(jnp.broadcast_to(col, col.shape[:2] + (128,)))
    row = jnp.where(
        lane == sub,
        a,
        jnp.where(lane == sub + 8, b, jnp.where(lane == sub + 16, c, 0.0)),
    )
    return jnp.sum(row, axis=1, keepdims=True)


def stats_col(row, sub, lane):
    spread = jnp.broadcast_to(row, (row.shape[0], 8, 128))
    mine = jnp.logical_and(lane < 24, lane % 8 == sub)
    return jnp.sum(jnp.where(mine, spread, 0.0), axis=2, keepdims=True)


def partial_body(
    mig, lens, table, swapped, x1, z1, dt1, b1, c1, q1, kv1, state, cache,
    rate, bias, skip, x2, z2, dt2, b2, c2, q2, kv2,
    blocks, gated, leaving,
    q8, kv16, x8, z8, d8, b8, c8, scr,
):
    slot = slot_of(mig)
    inst = lax.axis_index("inst")
    tp = lax.axis_index("tp")
    cols = group_cols()
    sw = swapped[:SWAP, :].astype(F32)

    def rows8(scr, one, two, moved):
        n = one.shape[-1]
        scr[...] = jnp.zeros_like(scr)
        scr[0:3, :n] = one.astype(F32)
        scr[3:6, :n] = jnp.where(iota((3, n), 0) == slot, moved, two.astype(F32))
        return scr[...]

    q8[6:8, :] = jnp.zeros_like(q8[6:8, :])
    q8[0:3, :] = q1[...].astype(F32)
    q8[3:6, :] = q2[...].astype(F32)
    rows3 = iota((3, 128), 0) == slot
    for a in range(QHEADS):
        at = slice(a * QDIM, (a + 1) * QDIM)
        q8[3:6, at] = jnp.where(rows3, sw[a : a + 1], q8[3:6, at])
    kv16[...] = jnp.zeros_like(kv16)
    kv16[0:3, :] = kv1[...].astype(F32)
    kv16[3:6, :] = kv2[...].astype(F32)
    for a in range(2 * KVHEADS):
        at = slice(a * QDIM, (a + 1) * QDIM)
        kv16[3:6, at] = jnp.where(rows3, sw[KV + a : KV + a + 1], kv16[3:6, at])

    xx = rows8(x8, x1[...], x2[...], flat(sw[X2 : X2 + 4]))
    zz = rows8(z8, z1[...], z2[...], flat(sw[Z2 : Z2 + 4]))
    bb = rows8(b8, b1[:, cols], b2[:, cols], flat(sw[B2 : B2 + 2]))
    cc = rows8(c8, c1[:, cols], c2[:, cols], flat(sw[C2 : C2 + 2]))
    dd = rows8(d8, dt1[...], dt2[...], sw[D2 : D2 + 1, :HEADS])
    dt = softplus(expand(dd, 8) + expand(bias[...], 1))
    decay = jnp.exp(-dt * expand(rate[...], 1))
    read = jnp.zeros((8, COLS), F32)
    row256 = iota((8, STATE), 0)
    for r in range(REQ):
        ch = jnp.where(jnp.logical_or(row256 == r, row256 == r + 3), cc, 0.0).astype(BF16)
        for part in hi_lo(state[r].reshape(COLS, STATE)):
            read += lax.dot_general(ch, part, NT, preferred_element_type=F32)
    store_states(leaving, MOVED, state[slot, HALF:])
    pushed = dt * xx
    same = jnp.sum(bb * cc, axis=1, keepdims=True)
    cross = jnp.sum(pltpu.roll(bb, 3, 0) * cc, axis=1, keepdims=True)
    first = pltpu.roll(decay, 3, 0) * read + pltpu.roll(pushed, 3, 0) * cross
    row = iota((8, COLS), 0)
    y = decay * jnp.where(row >= 3, first, read) + pushed * same + expand(skip[...], 1) * xx
    g = y * silu(zz)
    gated[...] = g
    g = jnp.sum(jnp.where(row == slot + 3, g, 0.0), axis=0, keepdims=True)
    hi = g.astype(BF16).astype(F32)
    for k in range(4):
        piece = slice(k * 128, (k + 1) * 128)
        scr[GHI + k : GHI + k + 1, :] = hi[:, piece]
        scr[GLO + k : GLO + k + 1, :] = (g - hi)[:, piece]

    lane = iota((1, KEYS + EXTRA), 1)
    owner = jnp.full(lane.shape, -1, I32)
    ok = jnp.zeros(lane.shape, I32)
    late = jnp.logical_and(lane >= KEYS + REQ, lane < KEYS + 2 * REQ)
    for r in range(REQ):
        length = lens[inst * REQ + r]
        for p in range(PP):
            at = (lane // PAGE) == table[r, p]
            pos = tp * SPAN + p * PAGE + lane % PAGE
            owner = jnp.where(at, r, owner)
            ok = jnp.where(jnp.logical_and(at, pos < length), 1, ok)
        for e, pos in ((r, length), (r + REQ, length + 1)):
            at = lane == KEYS + e
            owner = jnp.where(at, r, owner)
            ok = jnp.where(jnp.logical_and(at, pos // SPAN == tp), 1, ok)
    row = iota((8, KEYS + EXTRA), 0)
    mine = jnp.where(row < 3, row, jnp.where(row < 6, row - 3, -2))
    valid = (mine == owner) & (ok == 1) & ((row >= 3) | jnp.logical_not(late))
    valid = jnp.broadcast_to(valid.astype(F32)[None], (QPK, 8, KEYS + EXTRA)) > 0.0
    sub = iota((QPK, 8, 128), 1)
    lane3 = iota((QPK, 8, 128), 2)
    lane2 = iota((QPK, 128), 1)
    extra = kv16[...].astype(BF16)
    stats = jnp.zeros((QPK, 128), F32)
    for k in range(KVHEADS):
        qk = jnp.concatenate(
            [q8[:, (k * QPK + h) * QDIM : (k * QPK + h + 1) * QDIM] for h in range(QPK)], axis=0
        ).astype(BF16)
        kcols = slice(k * QDIM, (k + 1) * QDIM)
        vcols = slice((KVHEADS + k) * QDIM, (KVHEADS + k + 1) * QDIM)
        keys = jnp.concatenate([cache[:, :, kcols].reshape(KEYS, QDIM), extra[:, kcols]], axis=0)
        vals = jnp.concatenate([cache[:, :, vcols].reshape(KEYS, QDIM), extra[:, vcols]], axis=0)
        s = lax.dot_general(qk, keys, NT, preferred_element_type=F32) * SCALE
        s = jnp.where(valid, s.reshape(QPK, 8, KEYS + EXTRA), NEG)
        top = jnp.max(s, axis=2, keepdims=True)
        w = jnp.where(valid, jnp.exp(s - top), 0.0).astype(BF16)
        total = jnp.sum(w.astype(F32), axis=2, keepdims=True)
        acc = jnp.dot(w.reshape(QPK * 8, KEYS + EXTRA), vals, preferred_element_type=F32)
        some = total > 0.0
        safe = jnp.where(some, total, 1.0)
        lse = jnp.where(some, top + jnp.log(safe), NEG)
        o = acc.reshape(QPK, 8, QDIM) / safe
        out = jnp.where(sub == 6, stats_row(lse, sub, lane3), o)
        blocks[k] = out.reshape(QPK * 8, QDIM).astype(BF16)
        gone = sub == slot + 3
        scr[k * QPK : (k + 1) * QPK, :] = jnp.sum(jnp.where(gone, o, 0.0), axis=1)
        a, b, c = split3(jnp.sum(jnp.where(gone, lse, 0.0), axis=1))
        stats = jnp.where(lane2 == 3 * k, a, stats)
        stats = jnp.where(lane2 == 3 * k + 1, b, stats)
        stats = jnp.where(lane2 == 3 * k + 2, c, stats)
    scr[LSE : LSE + QPK, :] = stats
    leaving[:MOVED, :] = scr[...].astype(BF16)


def partials(mig, lens, table, swapped, *rest):
    return call(
        partial_body,
        (
            like(KVHEADS, QPK * 8, QDIM),
            like(8, COLS, dtype=F32),
            like(MOVED + STATE_ROWS, 128),
        ),
        scalars(3) + here(1) + [whole(a) for a in rest],
        tuple(here(3)),
        [
            VMEM((8, QHEADS * QDIM), F32),
            VMEM((EXTRA, KVW), F32),
            VMEM((8, COLS), F32),
            VMEM((8, COLS), F32),
            VMEM((8, 128), F32),
            VMEM((8, STATE), F32),
            VMEM((8, STATE), F32),
            VMEM((MOVED, 128), F32),
        ],
        name="partials",
    )(mig, lens, table, swapped, *rest)


def insert_body(mig, blocks, gated, moved, out, gated_out):
    slot = slot_of(mig)
    sub = iota((QPK, 8, 128), 1)
    lane = iota((QPK, 8, 128), 2)
    mv = moved[:MOVED, :].astype(F32)
    g = flat(mv[GHI : GHI + 4] + mv[GLO : GLO + 4])
    g = jnp.where(iota((8, COLS), 0) == slot + 3, g, gated[...])
    gated_out[...] = g
    squares = jnp.sum(g * g, axis=1, keepdims=True)
    sq_row = stats_row(squares[None], sub[:1], lane[:1])
    stats = mv[LSE : LSE + QPK]
    lane2 = iota((QPK, 128), 1)
    mine = jnp.logical_and(lane < 24, lane % 8 == slot + 3)
    for k in range(KVHEADS):
        lse = jnp.where(lane2 // 3 == k, stats, 0.0)
        lse = jnp.sum(lse, axis=1, keepdims=True)[:, None, :]
        a, b, c = split3(jnp.broadcast_to(lse, (QPK, 8, 128)))
        terms = jnp.where(lane < 8, a, jnp.where(lane < 16, b, c))
        v = blocks[k].astype(F32).reshape(QPK, 8, 128)
        v = jnp.where(sub == slot + 3, mv[k * QPK : (k + 1) * QPK][:, None, :], v)
        v = jnp.where(jnp.logical_and(sub == 6, mine), terms, v)
        v = jnp.where(sub == 7, sq_row, v)
        v = v.reshape(QPK * 8, 128).astype(BF16)
        for z in range(2):
            out[k // 2 * 4 + z * 2 + k % 2] = v


def insert(mig, blocks, gated, moved):
    return call(
        insert_body,
        (like(2 * KVHEADS, QPK * 8, QDIM), like(8, COLS, dtype=F32)),
        scalars(1) + here(3),
        tuple(here(2)),
        name="insert",
    )(mig, blocks, gated, moved)


def finish_body(recv, gated, gain, blocks, m1, m2, scr):
    x = lax.axis_index("tp") // 4
    sub = iota((QPK, 8, 128), 1)
    lane = iota((QPK, 8, 128), 2)
    n = recv.shape[0]
    lses = [stats_col(recv[j].astype(F32).reshape(QPK, 8, 128)[:, 6:7], sub, lane) for j in range(n)]
    top = functools.reduce(jnp.maximum, lses)
    total = jnp.zeros_like(top)
    acc = jnp.zeros((QPK, 8, 128), F32)
    for j in range(n):
        w = jnp.exp(lses[j] - top)
        total += w
        acc += w * recv[j].astype(F32).reshape(QPK, 8, 128)
    o = (acc / total).reshape(QPK * 8, 128).astype(BF16)
    for k in range(KVHEADS):
        blocks[k] = o

    rows = recv[4 * x].astype(F32)[7:8]
    for j in range(1, 4):
        rows += recv[4 * x + j].astype(F32)[7:8]
    squares = stats_col(rows[None], sub[:1], lane[:1])[0]
    scr[...] = gated[...] * lax.rsqrt(squares * (1.0 / NORM) + 1e-05) * gain[...]
    m1[...] = scr[0:3, :].astype(BF16)
    m2[...] = scr[3:6, :].astype(BF16)


def finish(recv, gated, gain):
    return call(
        finish_body,
        (like(KVHEADS, QPK * 8, 128), like(REQ, COLS), like(REQ, COLS)),
        here(2) + [whole(gain)],
        tuple(here(3)),
        [VMEM((8, COLS), F32)],
        name="finish",
    )(recv, gated, gain)


def spread_body(recv, a1, a2, scr):
    for k in range(KVHEADS):
        rows = recv[k].astype(F32)
        for h in range(QPK):
            at = (k * QPK + h) * QDIM
            scr[:, at : at + QDIM] = rows[h * 8 : (h + 1) * 8]
    a1[...] = scr[0:3, :].astype(BF16)
    a2[...] = scr[3:6, :].astype(BF16)


def spread(recv):
    n = QHEADS * QDIM
    return call(
        spread_body,
        (like(REQ, n),) * 2,
        here(1),
        tuple(here(2)),
        [VMEM((8, n), F32)],
        name="spread",
    )(recv)


def update_body(mig, swapped, moved, x1, dt1, b1, rate, bias, x2, dt2, b2, state, out, x8, d8, b8):
    slot = slot_of(mig)
    r = pl.program_id(0)
    cols = group_cols()
    sw = swapped[:SWAP, :].astype(F32)

    def rows8(scr, one, two, moved):
        n = one.shape[-1]
        scr[...] = jnp.zeros_like(scr)
        scr[0:3, :n] = jnp.where(iota((3, n), 0) == slot, moved, one.astype(F32))
        scr[3:6, :n] = two.astype(F32)
        return scr[...]

    xx = rows8(x8, x1[...], x2[...], flat(sw[X1 : X1 + 4]))
    bb = rows8(b8, b1[:, cols], b2[:, cols], flat(sw[B1 : B1 + 2]))
    dd = rows8(d8, dt1[...], dt2[...], sw[D1 : D1 + 1, :HEADS])
    dt = softplus(expand(dd, 8) + expand(bias[...], 1))
    decay = jnp.exp(-dt * expand(rate[...], 1))
    pushed = dt * xx
    later = pltpu.roll(decay, 5, 0)
    row = iota((8, COLS), 0)
    u = jnp.where(row < 3, pushed * later, pushed)
    both = jnp.sum(jnp.where(row == r, decay * later, 0.0), axis=0, keepdims=True)
    mine = jnp.logical_or(row == r, row == r + 3)
    bh = bb.astype(BF16)
    add = jnp.zeros((COLS, STATE), F32)
    for part in hi_lo(jnp.where(mine, u, 0.0)):
        add += lax.dot_general(part, bh, (((0,), (0,)), ((), ())), preferred_element_type=F32)
    new = r == slot
    for h in range(HEADS):
        if h < HALF:
            arrived = load_state(swapped, SWAP, h)
        else:
            arrived = load_state(moved, MOVED, h - HALF)
        s = jnp.where(new, arrived.astype(F32), state[0, h])
        d = both[:, h * HDIM : h * HDIM + 1]
        out[0, h] = d * s + add[h * HDIM : (h + 1) * HDIM]


def update(mig, swapped, moved, *rest):
    state = rest[-1]
    block = pl.BlockSpec((1,) + state.shape[1:], lambda r: (r, 0, 0, 0))
    return call(
        update_body,
        like(*state.shape, dtype=F32),
        scalars(1) + here(2) + [whole(a) for a in rest[:-1]] + [block],
        block,
        [VMEM((8, COLS), F32), VMEM((8, 128), F32), VMEM((8, STATE), F32)],
        grid=(REQ,),
        name="update",
    )(mig, swapped, moved, *rest)


PLANE = [[x * 4 + z * 2 + c for x in range(4) for c in range(2)] for z in range(2)]


def swap(m, v):
    return lax.ppermute(v, "inst", [(s, s ^ m) for s in range(lax.axis_size("inst"))])


def shards(
    x_one, z_one, dt_one, b_one, c_one, q_one, kv_one, state, cache, page_table,
    lengths, migration, decay_rate, dt_bias, skip_gain, norm_gain,
    x_two, z_two, dt_two, b_two, c_two, q_two, kv_two,
):
    rate, bias, skip, gain = decay_rate[None], dt_bias[None], skip_gain[None], norm_gain[None]
    which = migration[0, 1] - 1

    def by_partner(body, *operands):
        ways = range(1, lax.axis_size("inst"))
        return lax.switch(which, [functools.partial(body, m) for m in ways], *operands)

    payload = prepare(
        migration, x_one, dt_one, b_one, q_two, kv_two, x_two, z_two, dt_two, b_two, c_two, state
    )
    swapped = by_partner(swap, payload)
    blocks, gated, leaving = partials(
        migration, lengths, page_table, swapped,
        x_one, z_one, dt_one, b_one, c_one, q_one, kv_one, state, cache,
        rate, bias, skip, x_two, z_two, dt_two, b_two, c_two, q_two, kv_two,
    )
    moved = by_partner(swap, leaving)
    blocks, gated = insert(migration, blocks, gated, moved)
    recv = lax.all_to_all(blocks, "tp", 0, 0)
    blocks, mamba_one, mamba_two = finish(recv, gated, gain)
    recv = lax.all_to_all(blocks, "tp", 0, 0, axis_index_groups=PLANE)
    attn_one, attn_two = spread(recv)
    state_out = update(
        migration, swapped, moved, x_one, dt_one, b_one, rate, bias, x_two, dt_two, b_two, state
    )
    return mamba_one, attn_one, mamba_two, attn_two, state_out


def solution(mesh):
    row = P("inst", "tp")
    wide = P("inst", None)
    head = P("tp")
    states = P("inst", "tp", None, None)
    return jax.shard_map(
        shards,
        mesh=mesh,
        in_specs=(
            row, row, row, wide, wide, wide, wide, states, P("inst", None, "tp"), row,
            P(), P(), head, head, head, head, row, row, row, wide, wide, wide, wide,
        ),
        out_specs=(row, wide, row, wide, states),
        check_vma=False,
    )
```

```python
import functools

import jax
import jax.numpy as jnp
from jax import lax
from jax.experimental import pallas as pl
from jax.experimental.pallas import tpu as pltpu
from jax.sharding import PartitionSpec as P

F32 = jnp.float32
BF16 = jnp.bfloat16
I32 = jnp.int32

HPG = 32
QDIM = 128
STATE = 256
REQ = 3
HEADS = 8
HALF = HEADS // 2
HDIM = 64
COLS = HEADS * HDIM
STATE_ROWS = HALF * HDIM * 2
KVHEADS = 8
QPK = 8
QHEADS = KVHEADS * QPK
KVW = 2 * KVHEADS * QDIM
PAGE = 16
POOL = 12
PP = 4
SPAN = PP * PAGE
KEYS = POOL * PAGE
EXTRA = 16
NORM = HPG * HDIM
NEG = -1e30
SCALE = 1.0 / QDIM**0.5

KV = QHEADS
X2 = KV + 16
Z2 = X2 + 4
B2 = Z2 + 4
C2 = B2 + 2
D2 = C2 + 2
D1 = D2 + 1
X1 = D1 + 1
B1 = X1 + 4
SWAP = 112

LSE = QHEADS
GHI = LSE + 8
GLO = GHI + 4
MOVED = 80

VMEM = pltpu.VMEM
NT = (((1,), (1,)), ((), ()))


def iota(shape, dim):
    return lax.broadcasted_iota(I32, shape, dim)


def split3(v):
    a = v.astype(BF16).astype(F32)
    rest = v - a
    b = rest.astype(BF16).astype(F32)
    c = (rest - b).astype(BF16).astype(F32)
    return a, b, c


def store_states(out, at, v):
    n = HALF * HDIM
    v = v.reshape(n, STATE).astype(BF16)
    out[at : at + n, :] = v[:, :128]
    out[at + n : at + 2 * n, :] = v[:, 128:]


def load_state(ref, at, h):
    first = at + h * HDIM
    second = first + HALF * HDIM
    return jnp.concatenate([ref[first : first + HDIM, :], ref[second : second + HDIM, :]], axis=1)


def entry(mig, column, row):
    mine = jnp.logical_and(iota(mig.shape, 0) == column, iota(mig.shape, 1) == row)
    return jnp.sum(jnp.where(mine, mig[...], 0).astype(F32)).astype(I32)


def slot_of(mig):
    inst = lax.axis_index("inst")
    return entry(mig, 0, inst) - inst * REQ


def whole(a):
    return pl.BlockSpec(a.shape, lambda i: (0,) * a.ndim)


def here(n):
    return [pl.BlockSpec(memory_space=VMEM)] * n


def scalars(n):
    return [pl.BlockSpec(memory_space=pltpu.SMEM)] * n


def call(body, out_shape, in_specs, out_specs, scratch=(), grid=(1,), vmem=60, **kw):
    return pl.pallas_call(
        body,
        out_shape=out_shape,
        in_specs=in_specs,
        out_specs=out_specs,
        scratch_shapes=list(scratch),
        compiler_params=pltpu.CompilerParams(vmem_limit_bytes=vmem * 2**20),
        grid=grid,
        **kw,
    )


def like(*shape, dtype=BF16):
    return jax.ShapeDtypeStruct(shape, dtype)


def expand(per_head, rows):
    head = iota((rows, COLS), 1) // HDIM
    out = jnp.zeros((rows, COLS), F32)
    for h in range(HEADS):
        out = jnp.where(head == h, per_head[:, h : h + 1], out)
    return out


def flat(rows):
    return jnp.concatenate([rows[k : k + 1] for k in range(rows.shape[0])], axis=1)


def softplus(v):
    return jnp.maximum(v, 0.0) + jnp.log1p(jnp.exp(-jnp.abs(v)))


def silu(v):
    return v / (1.0 + jnp.exp(-v))


def group_cols():
    g = lax.axis_index("tp") * HEADS // HPG
    return pl.ds(pl.multiple_of(g * STATE, STATE), STATE)


def hi_lo(v):
    hi = v.astype(BF16)
    return hi, (v - hi.astype(F32)).astype(BF16)


def prepare_body(mig, x1, dt1, b1, q2, kv2, x2, z2, dt2, b2, c2, state, out, pairing, rows, held, sem):
    slot = slot_of(mig)
    copy = pltpu.make_async_copy(state.at[slot, :HALF], held, sem)
    copy.start()
    pairing[0] = entry(mig, 1, 0)

    def put(at, v):
        v = v.astype(F32)
        v = jnp.sum(jnp.where(iota(v.shape, 0) == slot, v, 0.0), axis=0, keepdims=True)
        width = min(v.shape[1], 128)
        for k in range(v.shape[1] // width):
            rows[at + k : at + k + 1, :width] = v[:, k * width : (k + 1) * width]

    cols = group_cols()
    rows[D2:, :] = jnp.zeros_like(rows[D2:, :])
    put(0, q2[...])
    put(KV, kv2[...])
    put(X2, x2[...])
    put(Z2, z2[...])
    put(B2, b2[:, cols])
    put(C2, c2[:, cols])
    put(D2, dt2[...])
    put(D1, dt1[...])
    put(X1, x1[...])
    put(B1, b1[:, cols])
    out[:SWAP, :] = rows[...].astype(BF16)
    copy.wait()
    store_states(out, SWAP, held[...])


def prepare(mig, *rest):
    return call(
        prepare_body,
        (like(SWAP + STATE_ROWS, 128), like(1, dtype=I32)),
        [whole(mig)] + [whole(a) for a in rest[:-1]] + [pl.BlockSpec(memory_space=pl.ANY)],
        (here(1)[0], scalars(1)[0]),
        [VMEM((SWAP, 128), F32), VMEM((HALF, HDIM, STATE), F32), pltpu.SemaphoreType.DMA],
        name="prepare",
    )(mig, *rest)


def stats_row(col, sub, lane):
    a, b, c = split3(jnp.broadcast_to(col, col.shape[:2] + (128,)))
    row = jnp.where(
        lane == sub,
        a,
        jnp.where(lane == sub + 8, b, jnp.where(lane == sub + 16, c, 0.0)),
    )
    return jnp.sum(row, axis=1, keepdims=True)


def stats_col(row, sub, lane):
    spread = jnp.broadcast_to(row, (row.shape[0], 8, 128))
    mine = jnp.logical_and(lane < 24, lane % 8 == sub)
    return jnp.sum(jnp.where(mine, spread, 0.0), axis=2, keepdims=True)


def partial_body(
    lens, table, mig, swapped, x1, z1, dt1, b1, c1, q1, kv1, state, cache,
    rate, bias, skip, x2, z2, dt2, b2, c2, q2, kv2,
    blocks, gated, leaving,
    q8, kv16, x8, z8, d8, b8, c8, scr,
):
    slot = slot_of(mig)
    inst = lax.axis_index("inst")
    tp = lax.axis_index("tp")
    cols = group_cols()
    sw = swapped[:SWAP, :].astype(F32)

    def rows8(scr, one, two, moved):
        n = one.shape[-1]
        scr[...] = jnp.zeros_like(scr)
        scr[0:3, :n] = one.astype(F32)
        scr[3:6, :n] = jnp.where(iota((3, n), 0) == slot, moved, two.astype(F32))
        return scr[...]

    q8[6:8, :] = jnp.zeros_like(q8[6:8, :])
    q8[0:3, :] = q1[...].astype(F32)
    q8[3:6, :] = q2[...].astype(F32)
    rows3 = iota((3, 128), 0) == slot
    for a in range(QHEADS):
        at = slice(a * QDIM, (a + 1) * QDIM)
        q8[3:6, at] = jnp.where(rows3, sw[a : a + 1], q8[3:6, at])
    kv16[...] = jnp.zeros_like(kv16)
    kv16[0:3, :] = kv1[...].astype(F32)
    kv16[3:6, :] = kv2[...].astype(F32)
    for a in range(2 * KVHEADS):
        at = slice(a * QDIM, (a + 1) * QDIM)
        kv16[3:6, at] = jnp.where(rows3, sw[KV + a : KV + a + 1], kv16[3:6, at])

    xx = rows8(x8, x1[...], x2[...], flat(sw[X2 : X2 + 4]))
    zz = rows8(z8, z1[...], z2[...], flat(sw[Z2 : Z2 + 4]))
    bb = rows8(b8, b1[:, cols], b2[:, cols], flat(sw[B2 : B2 + 2]))
    cc = rows8(c8, c1[:, cols], c2[:, cols], flat(sw[C2 : C2 + 2]))
    dd = rows8(d8, dt1[...], dt2[...], sw[D2 : D2 + 1, :HEADS])
    dt = softplus(expand(dd, 8) + expand(bias[...], 1))
    decay = jnp.exp(-dt * expand(rate[...], 1))
    read = jnp.zeros((8, COLS), F32)
    row256 = iota((8, STATE), 0)
    for r in range(REQ):
        ch = jnp.where(jnp.logical_or(row256 == r, row256 == r + 3), cc, 0.0).astype(BF16)
        for part in hi_lo(state[r].reshape(COLS, STATE)):
            read += lax.dot_general(ch, part, NT, preferred_element_type=F32)
    store_states(leaving, MOVED, state[slot, HALF:])
    pushed = dt * xx
    same = jnp.sum(bb * cc, axis=1, keepdims=True)
    cross = jnp.sum(pltpu.roll(bb, 3, 0) * cc, axis=1, keepdims=True)
    first = pltpu.roll(decay, 3, 0) * read + pltpu.roll(pushed, 3, 0) * cross
    row = iota((8, COLS), 0)
    y = decay * jnp.where(row >= 3, first, read) + pushed * same + expand(skip[...], 1) * xx
    g = y * silu(zz)
    gated[...] = g
    g = jnp.sum(jnp.where(row == slot + 3, g, 0.0), axis=0, keepdims=True)
    hi = g.astype(BF16).astype(F32)
    for k in range(4):
        piece = slice(k * 128, (k + 1) * 128)
        scr[GHI + k : GHI + k + 1, :] = hi[:, piece]
        scr[GLO + k : GLO + k + 1, :] = (g - hi)[:, piece]

    lane = iota((1, KEYS + EXTRA), 1)
    owner = jnp.full(lane.shape, -1, I32)
    ok = jnp.zeros(lane.shape, I32)
    late = jnp.logical_and(lane >= KEYS + REQ, lane < KEYS + 2 * REQ)
    for r in range(REQ):
        length = lens[inst * REQ + r]
        for p in range(PP):
            at = (lane // PAGE) == table[r, p]
            pos = tp * SPAN + p * PAGE + lane % PAGE
            owner = jnp.where(at, r, owner)
            ok = jnp.where(jnp.logical_and(at, pos < length), 1, ok)
        for e, pos in ((r, length), (r + REQ, length + 1)):
            at = lane == KEYS + e
            owner = jnp.where(at, r, owner)
            ok = jnp.where(jnp.logical_and(at, pos // SPAN == tp), 1, ok)
    row = iota((8, KEYS + EXTRA), 0)
    mine = jnp.where(row < 3, row, jnp.where(row < 6, row - 3, -2))
    valid = (mine == owner) & (ok == 1) & ((row >= 3) | jnp.logical_not(late))
    valid = jnp.broadcast_to(valid.astype(F32)[None], (QPK, 8, KEYS + EXTRA)) > 0.0
    sub = iota((QPK, 8, 128), 1)
    lane3 = iota((QPK, 8, 128), 2)
    lane2 = iota((QPK, 128), 1)
    extra = kv16[...].astype(BF16)
    stats = jnp.zeros((QPK, 128), F32)
    for k in range(KVHEADS):
        qk = jnp.concatenate(
            [q8[:, (k * QPK + h) * QDIM : (k * QPK + h + 1) * QDIM] for h in range(QPK)], axis=0
        ).astype(BF16)
        kcols = slice(k * QDIM, (k + 1) * QDIM)
        vcols = slice((KVHEADS + k) * QDIM, (KVHEADS + k + 1) * QDIM)
        keys = jnp.concatenate([cache[:, :, kcols].reshape(KEYS, QDIM), extra[:, kcols]], axis=0)
        vals = jnp.concatenate([cache[:, :, vcols].reshape(KEYS, QDIM), extra[:, vcols]], axis=0)
        s = lax.dot_general(qk, keys, NT, preferred_element_type=F32) * SCALE
        s = jnp.where(valid, s.reshape(QPK, 8, KEYS + EXTRA), NEG)
        top = jnp.max(s, axis=2, keepdims=True)
        w = jnp.where(valid, jnp.exp(s - top), 0.0).astype(BF16)
        total = jnp.sum(w.astype(F32), axis=2, keepdims=True)
        acc = jnp.dot(w.reshape(QPK * 8, KEYS + EXTRA), vals, preferred_element_type=F32)
        some = total > 0.0
        safe = jnp.where(some, total, 1.0)
        lse = jnp.where(some, top + jnp.log(safe), NEG)
        o = acc.reshape(QPK, 8, QDIM) / safe
        out = jnp.where(sub == 6, stats_row(lse, sub, lane3), o)
        blocks[k] = out.reshape(QPK * 8, QDIM).astype(BF16)
        gone = sub == slot + 3
        scr[k * QPK : (k + 1) * QPK, :] = jnp.sum(jnp.where(gone, o, 0.0), axis=1)
        a, b, c = split3(jnp.sum(jnp.where(gone, lse, 0.0), axis=1))
        stats = jnp.where(lane2 == 3 * k, a, stats)
        stats = jnp.where(lane2 == 3 * k + 1, b, stats)
        stats = jnp.where(lane2 == 3 * k + 2, c, stats)
    scr[LSE : LSE + QPK, :] = stats
    leaving[:MOVED, :] = scr[...].astype(BF16)


def partials(lens, table, mig, swapped, *rest):
    return call(
        partial_body,
        (
            like(KVHEADS, QPK * 8, QDIM),
            like(8, COLS, dtype=F32),
            like(MOVED + STATE_ROWS, 128),
        ),
        scalars(2) + [whole(mig)] + here(1) + [whole(a) for a in rest],
        tuple(here(3)),
        [
            VMEM((8, QHEADS * QDIM), F32),
            VMEM((EXTRA, KVW), F32),
            VMEM((8, COLS), F32),
            VMEM((8, COLS), F32),
            VMEM((8, 128), F32),
            VMEM((8, STATE), F32),
            VMEM((8, STATE), F32),
            VMEM((MOVED, 128), F32),
        ],
        name="partials",
    )(lens, table, mig, swapped, *rest)


def insert_body(mig, blocks, gated, moved, out, gated_out):
    slot = slot_of(mig)
    sub = iota((QPK, 8, 128), 1)
    lane = iota((QPK, 8, 128), 2)
    mv = moved[:MOVED, :].astype(F32)
    g = flat(mv[GHI : GHI + 4] + mv[GLO : GLO + 4])
    g = jnp.where(iota((8, COLS), 0) == slot + 3, g, gated[...])
    gated_out[...] = g
    squares = jnp.sum(g * g, axis=1, keepdims=True)
    sq_row = stats_row(squares[None], sub[:1], lane[:1])
    stats = mv[LSE : LSE + QPK]
    lane2 = iota((QPK, 128), 1)
    mine = jnp.logical_and(lane < 24, lane % 8 == slot + 3)
    for k in range(KVHEADS):
        lse = jnp.where(lane2 // 3 == k, stats, 0.0)
        lse = jnp.sum(lse, axis=1, keepdims=True)[:, None, :]
        a, b, c = split3(jnp.broadcast_to(lse, (QPK, 8, 128)))
        terms = jnp.where(lane < 8, a, jnp.where(lane < 16, b, c))
        v = blocks[k].astype(F32).reshape(QPK, 8, 128)
        v = jnp.where(sub == slot + 3, mv[k * QPK : (k + 1) * QPK][:, None, :], v)
        v = jnp.where(jnp.logical_and(sub == 6, mine), terms, v)
        v = jnp.where(sub == 7, sq_row, v)
        v = v.reshape(QPK * 8, 128).astype(BF16)
        for z in range(2):
            out[k // 2 * 4 + z * 2 + k % 2] = v


def insert(mig, blocks, gated, moved):
    return call(
        insert_body,
        (like(2 * KVHEADS, QPK * 8, QDIM), like(8, COLS, dtype=F32)),
        [whole(mig)] + here(3),
        tuple(here(2)),
        name="insert",
    )(mig, blocks, gated, moved)


def finish_body(recv, gated, gain, blocks, m1, m2, scr):
    x = lax.axis_index("tp") // 4
    sub = iota((QPK, 8, 128), 1)
    lane = iota((QPK, 8, 128), 2)
    n = recv.shape[0]
    lses = [stats_col(recv[j].astype(F32).reshape(QPK, 8, 128)[:, 6:7], sub, lane) for j in range(n)]
    top = functools.reduce(jnp.maximum, lses)
    total = jnp.zeros_like(top)
    acc = jnp.zeros((QPK, 8, 128), F32)
    for j in range(n):
        w = jnp.exp(lses[j] - top)
        total += w
        acc += w * recv[j].astype(F32).reshape(QPK, 8, 128)
    o = (acc / total).reshape(QPK * 8, 128).astype(BF16)
    for k in range(KVHEADS):
        blocks[k] = o

    rows = recv[4 * x].astype(F32)[7:8]
    for j in range(1, 4):
        rows += recv[4 * x + j].astype(F32)[7:8]
    squares = stats_col(rows[None], sub[:1], lane[:1])[0]
    scr[...] = gated[...] * lax.rsqrt(squares * (1.0 / NORM) + 1e-05) * gain[...]
    m1[...] = scr[0:3, :].astype(BF16)
    m2[...] = scr[3:6, :].astype(BF16)


def finish(recv, gated, gain):
    return call(
        finish_body,
        (like(KVHEADS, QPK * 8, 128), like(REQ, COLS), like(REQ, COLS)),
        here(2) + [whole(gain)],
        tuple(here(3)),
        [VMEM((8, COLS), F32)],
        name="finish",
    )(recv, gated, gain)


def spread_body(recv, a1, a2, scr):
    for k in range(KVHEADS):
        rows = recv[k].astype(F32)
        for h in range(QPK):
            at = (k * QPK + h) * QDIM
            scr[:, at : at + QDIM] = rows[h * 8 : (h + 1) * 8]
    a1[...] = scr[0:3, :].astype(BF16)
    a2[...] = scr[3:6, :].astype(BF16)


def spread(recv):
    n = QHEADS * QDIM
    return call(
        spread_body,
        (like(REQ, n),) * 2,
        here(1),
        tuple(here(2)),
        [VMEM((8, n), F32)],
        vmem=8,
        name="spread",
    )(recv)


def update_body(mig, swapped, moved, x1, dt1, b1, rate, bias, x2, dt2, b2, state, out, x8, d8, b8):
    slot = slot_of(mig)
    r = pl.program_id(0)
    cols = group_cols()
    sw = swapped[:SWAP, :].astype(F32)

    def rows8(scr, one, two, moved):
        n = one.shape[-1]
        scr[...] = jnp.zeros_like(scr)
        scr[0:3, :n] = jnp.where(iota((3, n), 0) == slot, moved, one.astype(F32))
        scr[3:6, :n] = two.astype(F32)
        return scr[...]

    xx = rows8(x8, x1[...], x2[...], flat(sw[X1 : X1 + 4]))
    bb = rows8(b8, b1[:, cols], b2[:, cols], flat(sw[B1 : B1 + 2]))
    dd = rows8(d8, dt1[...], dt2[...], sw[D1 : D1 + 1, :HEADS])
    dt = softplus(expand(dd, 8) + expand(bias[...], 1))
    decay = jnp.exp(-dt * expand(rate[...], 1))
    pushed = dt * xx
    later = pltpu.roll(decay, 5, 0)
    row = iota((8, COLS), 0)
    u = jnp.where(row < 3, pushed * later, pushed)
    both = jnp.sum(jnp.where(row == r, decay * later, 0.0), axis=0, keepdims=True)
    mine = jnp.logical_or(row == r, row == r + 3)
    bh = bb.astype(BF16)
    add = jnp.zeros((COLS, STATE), F32)
    for part in hi_lo(jnp.where(mine, u, 0.0)):
        add += lax.dot_general(part, bh, (((0,), (0,)), ((), ())), preferred_element_type=F32)
    new = r == slot
    for h in range(HEADS):
        if h < HALF:
            arrived = load_state(swapped, SWAP, h)
        else:
            arrived = load_state(moved, MOVED, h - HALF)
        s = jnp.where(new, arrived.astype(F32), state[0, h])
        d = both[:, h * HDIM : h * HDIM + 1]
        out[0, h] = d * s + add[h * HDIM : (h + 1) * HDIM]


def update(mig, swapped, moved, *rest):
    state = rest[-1]
    block = pl.BlockSpec((1,) + state.shape[1:], lambda r: (r, 0, 0, 0))
    return call(
        update_body,
        like(*state.shape, dtype=F32),
        [whole(mig)] + here(2) + [whole(a) for a in rest[:-1]] + [block],
        block,
        [VMEM((8, COLS), F32), VMEM((8, 128), F32), VMEM((8, STATE), F32)],
        grid=(REQ,),
        name="update",
    )(mig, swapped, moved, *rest)


PLANE = [[x * 4 + z * 2 + c for x in range(4) for c in range(2)] for z in range(2)]


def swap(m, v):
    return lax.ppermute(v, "inst", [(s, s ^ m) for s in range(lax.axis_size("inst"))])


def shards(
    x_one, z_one, dt_one, b_one, c_one, q_one, kv_one, state, cache, page_table,
    lengths, migration, decay_rate, dt_bias, skip_gain, norm_gain,
    x_two, z_two, dt_two, b_two, c_two, q_two, kv_two,
):
    rate, bias, skip, gain = decay_rate[None], dt_bias[None], skip_gain[None], norm_gain[None]
    migration = migration.T

    def by_partner(body, *operands):
        ways = range(1, lax.axis_size("inst"))
        return lax.switch(pairing - 1, [functools.partial(body, m) for m in ways], *operands)

    payload, pairing = prepare(
        migration, x_one, dt_one, b_one, q_two, kv_two, x_two, z_two, dt_two, b_two, c_two, state
    )
    pairing = pairing[0]
    swapped = by_partner(swap, payload)
    blocks, gated, leaving = partials(
        lengths, page_table, migration, swapped,
        x_one, z_one, dt_one, b_one, c_one, q_one, kv_one, state, cache,
        rate, bias, skip, x_two, z_two, dt_two, b_two, c_two, q_two, kv_two,
    )
    moved = by_partner(swap, leaving)
    blocks, gated = insert(migration, blocks, gated, moved)
    recv = lax.all_to_all(blocks, "tp", 0, 0)
    blocks, mamba_one, mamba_two = finish(recv, gated, gain)
    recv = lax.all_to_all(blocks, "tp", 0, 0, axis_index_groups=PLANE)
    attn_one, attn_two = spread(recv)
    state_out = update(
        migration, swapped, moved, x_one, dt_one, b_one, rate, bias, x_two, dt_two, b_two, state
    )
    return mamba_one, attn_one, mamba_two, attn_two, state_out


def solution(mesh):
    row = P("inst", "tp")
    wide = P("inst", None)
    head = P("tp")
    states = P("inst", "tp", None, None)
    return jax.shard_map(
        shards,
        mesh=mesh,
        in_specs=(
            row, row, row, wide, wide, wide, wide, states, P("inst", None, "tp"), row,
            P(), P(), head, head, head, head, row, row, row, wide, wide, wide, wide,
        ),
        out_specs=(row, wide, row, wide, states),
        check_vma=False,
    )
```

```python
import functools

import jax
import jax.numpy as jnp
from jax import lax
from jax.experimental import pallas as pl
from jax.experimental.pallas import tpu as pltpu
from jax.sharding import PartitionSpec as P

F32 = jnp.float32
BF16 = jnp.bfloat16
I32 = jnp.int32

HPG = 32
QDIM = 128
STATE = 256
REQ = 3
HEADS = 8
HALF = HEADS // 2
HDIM = 64
COLS = HEADS * HDIM
STATE_ROWS = HALF * HDIM * 2
KVHEADS = 8
QPK = 8
QHEADS = KVHEADS * QPK
KVW = 2 * KVHEADS * QDIM
PAGE = 16
POOL = 12
PP = 4
SPAN = PP * PAGE
KEYS = POOL * PAGE
EXTRA = 16
NORM = HPG * HDIM
NEG = -1e30
SCALE = 1.0 / QDIM**0.5

KV = QHEADS
X2 = KV + 16
Z2 = X2 + 4
B2 = Z2 + 4
C2 = B2 + 2
D2 = C2 + 2
D1 = D2 + 1
X1 = D1 + 1
B1 = X1 + 4
SWAP = 112

LSE = QHEADS
GHI = LSE + 8
GLO = GHI + 4
MOVED = 80

VMEM = pltpu.VMEM
NT = (((1,), (1,)), ((), ()))


def iota(shape, dim):
    return lax.broadcasted_iota(I32, shape, dim)


def split3(v):
    a = v.astype(BF16).astype(F32)
    rest = v - a
    b = rest.astype(BF16).astype(F32)
    c = (rest - b).astype(BF16).astype(F32)
    return a, b, c


def store_states(out, at, v):
    n = HALF * HDIM
    v = v.reshape(n, STATE).astype(BF16)
    out[at : at + n, :] = v[:, :128]
    out[at + n : at + 2 * n, :] = v[:, 128:]


def load_state(ref, at, h):
    first = at + h * HDIM
    second = first + HALF * HDIM
    return jnp.concatenate([ref[first : first + HDIM, :], ref[second : second + HDIM, :]], axis=1)


def entry(mig, column, row):
    mine = jnp.logical_and(iota(mig.shape, 0) == column, iota(mig.shape, 1) == row)
    return jnp.sum(jnp.where(mine, mig[...], 0).astype(F32)).astype(I32)


def pack_rows(v):
    hi = v.astype(BF16).astype(F32)
    parts = [t[:, k * 128 : (k + 1) * 128] for t in (hi, v - hi) for k in range(COLS // 128)]
    return jnp.concatenate(parts, axis=0).astype(BF16)


def unpack_rows(v):
    v = v.astype(F32)
    v = v[:32] + v[32:]
    return jnp.concatenate([v[8 * k : 8 * k + 8] for k in range(COLS // 128)], axis=1)


def slot_of(mig):
    inst = lax.axis_index("inst")
    return entry(mig, 0, inst) - inst * REQ


def whole(a):
    return pl.BlockSpec(a.shape, lambda i: (0,) * a.ndim)


def here(n):
    return [pl.BlockSpec(memory_space=VMEM)] * n


def scalars(n):
    return [pl.BlockSpec(memory_space=pltpu.SMEM)] * n


def call(body, out_shape, in_specs, out_specs, scratch=(), grid=(1,), vmem=60, **kw):
    return pl.pallas_call(
        body,
        out_shape=out_shape,
        in_specs=in_specs,
        out_specs=out_specs,
        scratch_shapes=list(scratch),
        compiler_params=pltpu.CompilerParams(vmem_limit_bytes=vmem * 2**20),
        grid=grid,
        **kw,
    )


def like(*shape, dtype=BF16):
    return jax.ShapeDtypeStruct(shape, dtype)


def expand(per_head, rows):
    head = iota((rows, COLS), 1) // HDIM
    out = jnp.zeros((rows, COLS), F32)
    for h in range(HEADS):
        out = jnp.where(head == h, per_head[:, h : h + 1], out)
    return out


def flat(rows):
    return jnp.concatenate([rows[k : k + 1] for k in range(rows.shape[0])], axis=1)


def softplus(v):
    return jnp.maximum(v, 0.0) + jnp.log1p(jnp.exp(-jnp.abs(v)))


def silu(v):
    return v / (1.0 + jnp.exp(-v))


def group_cols():
    g = lax.axis_index("tp") * HEADS // HPG
    return pl.ds(pl.multiple_of(g * STATE, STATE), STATE)


def hi_lo(v):
    hi = v.astype(BF16)
    return hi, (v - hi.astype(F32)).astype(BF16)


def prepare_body(mig, x1, dt1, b1, q2, kv2, x2, z2, dt2, b2, c2, state, out, pairing, rows, held, sem):
    slot = slot_of(mig)
    copy = pltpu.make_async_copy(state.at[slot, :HALF], held, sem)
    copy.start()
    pairing[0] = entry(mig, 1, 0)

    def put(at, v):
        v = v.astype(F32)
        v = jnp.sum(jnp.where(iota(v.shape, 0) == slot, v, 0.0), axis=0, keepdims=True)
        width = min(v.shape[1], 128)
        for k in range(v.shape[1] // width):
            rows[at + k : at + k + 1, :width] = v[:, k * width : (k + 1) * width]

    cols = group_cols()
    rows[D2:, :] = jnp.zeros_like(rows[D2:, :])
    put(0, q2[...])
    put(KV, kv2[...])
    put(X2, x2[...])
    put(Z2, z2[...])
    put(B2, b2[:, cols])
    put(C2, c2[:, cols])
    put(D2, dt2[...])
    put(D1, dt1[...])
    put(X1, x1[...])
    put(B1, b1[:, cols])
    out[:SWAP, :] = rows[...].astype(BF16)
    copy.wait()
    store_states(out, SWAP, held[...])


def prepare(mig, *rest):
    return call(
        prepare_body,
        (like(SWAP + STATE_ROWS, 128), like(1, dtype=I32)),
        [whole(mig)] + [whole(a) for a in rest[:-1]] + [pl.BlockSpec(memory_space=pl.ANY)],
        (here(1)[0], scalars(1)[0]),
        [VMEM((SWAP, 128), F32), VMEM((HALF, HDIM, STATE), F32), pltpu.SemaphoreType.DMA],
        name="prepare",
    )(mig, *rest)


def stats_row(col, sub, lane):
    a, b, c = split3(jnp.broadcast_to(col, col.shape[:2] + (128,)))
    row = jnp.where(
        lane == sub,
        a,
        jnp.where(lane == sub + 8, b, jnp.where(lane == sub + 16, c, 0.0)),
    )
    return jnp.sum(row, axis=1, keepdims=True)


def stats_col(row, sub, lane):
    spread = jnp.broadcast_to(row, (row.shape[0], 8, 128))
    mine = jnp.logical_and(lane < 24, lane % 8 == sub)
    return jnp.sum(jnp.where(mine, spread, 0.0), axis=2, keepdims=True)


def partial_body(
    lens, table, mig, swapped, x1, z1, dt1, b1, c1, q1, kv1, state, cache,
    rate, bias, skip, x2, z2, dt2, b2, c2, q2, kv2,
    blocks, leaving,
    q8, kv16, x8, z8, d8, b8, c8, scr,
):
    slot = slot_of(mig)
    inst = lax.axis_index("inst")
    tp = lax.axis_index("tp")
    cols = group_cols()
    sw = swapped[:SWAP, :].astype(F32)

    def rows8(scr, one, two, moved):
        n = one.shape[-1]
        scr[...] = jnp.zeros_like(scr)
        scr[0:3, :n] = one.astype(F32)
        scr[3:6, :n] = jnp.where(iota((3, n), 0) == slot, moved, two.astype(F32))
        return scr[...]

    q8[6:8, :] = jnp.zeros_like(q8[6:8, :])
    q8[0:3, :] = q1[...].astype(F32)
    q8[3:6, :] = q2[...].astype(F32)
    rows3 = iota((3, 128), 0) == slot
    for a in range(QHEADS):
        at = slice(a * QDIM, (a + 1) * QDIM)
        q8[3:6, at] = jnp.where(rows3, sw[a : a + 1], q8[3:6, at])
    kv16[...] = jnp.zeros_like(kv16)
    kv16[0:3, :] = kv1[...].astype(F32)
    kv16[3:6, :] = kv2[...].astype(F32)
    for a in range(2 * KVHEADS):
        at = slice(a * QDIM, (a + 1) * QDIM)
        kv16[3:6, at] = jnp.where(rows3, sw[KV + a : KV + a + 1], kv16[3:6, at])

    xx = rows8(x8, x1[...], x2[...], flat(sw[X2 : X2 + 4]))
    zz = rows8(z8, z1[...], z2[...], flat(sw[Z2 : Z2 + 4]))
    bb = rows8(b8, b1[:, cols], b2[:, cols], flat(sw[B2 : B2 + 2]))
    cc = rows8(c8, c1[:, cols], c2[:, cols], flat(sw[C2 : C2 + 2]))
    dd = rows8(d8, dt1[...], dt2[...], sw[D2 : D2 + 1, :HEADS])
    dt = softplus(expand(dd, 8) + expand(bias[...], 1))
    decay = jnp.exp(-dt * expand(rate[...], 1))
    read = jnp.zeros((8, COLS), F32)
    row256 = iota((8, STATE), 0)
    for r in range(REQ):
        ch = jnp.where(jnp.logical_or(row256 == r, row256 == r + 3), cc, 0.0).astype(BF16)
        for part in hi_lo(state[r].reshape(COLS, STATE)):
            read += lax.dot_general(ch, part, NT, preferred_element_type=F32)
    store_states(leaving, MOVED, state[slot, HALF:])
    pushed = dt * xx
    same = jnp.sum(bb * cc, axis=1, keepdims=True)
    cross = jnp.sum(pltpu.roll(bb, 3, 0) * cc, axis=1, keepdims=True)
    first = pltpu.roll(decay, 3, 0) * read + pltpu.roll(pushed, 3, 0) * cross
    row = iota((8, COLS), 0)
    y = decay * jnp.where(row >= 3, first, read) + pushed * same + expand(skip[...], 1) * xx
    g = y * silu(zz)
    blocks[KVHEADS] = pack_rows(g)
    g = jnp.sum(jnp.where(row == slot + 3, g, 0.0), axis=0, keepdims=True)
    hi = g.astype(BF16).astype(F32)
    for k in range(4):
        piece = slice(k * 128, (k + 1) * 128)
        scr[GHI + k : GHI + k + 1, :] = hi[:, piece]
        scr[GLO + k : GLO + k + 1, :] = (g - hi)[:, piece]

    lane = iota((1, KEYS + EXTRA), 1)
    owner = jnp.full(lane.shape, -1, I32)
    ok = jnp.zeros(lane.shape, I32)
    late = jnp.logical_and(lane >= KEYS + REQ, lane < KEYS + 2 * REQ)
    for r in range(REQ):
        length = lens[inst * REQ + r]
        for p in range(PP):
            at = (lane // PAGE) == table[r, p]
            pos = tp * SPAN + p * PAGE + lane % PAGE
            owner = jnp.where(at, r, owner)
            ok = jnp.where(jnp.logical_and(at, pos < length), 1, ok)
        for e, pos in ((r, length), (r + REQ, length + 1)):
            at = lane == KEYS + e
            owner = jnp.where(at, r, owner)
            ok = jnp.where(jnp.logical_and(at, pos // SPAN == tp), 1, ok)
    row = iota((8, KEYS + EXTRA), 0)
    mine = jnp.where(row < 3, row, jnp.where(row < 6, row - 3, -2))
    valid = (mine == owner) & (ok == 1) & ((row >= 3) | jnp.logical_not(late))
    valid = jnp.broadcast_to(valid.astype(F32)[None], (QPK, 8, KEYS + EXTRA)) > 0.0
    sub = iota((QPK, 8, 128), 1)
    lane3 = iota((QPK, 8, 128), 2)
    lane2 = iota((QPK, 128), 1)
    extra = kv16[...].astype(BF16)
    stats = jnp.zeros((QPK, 128), F32)
    for k in range(KVHEADS):
        qk = jnp.concatenate(
            [q8[:, (k * QPK + h) * QDIM : (k * QPK + h + 1) * QDIM] for h in range(QPK)], axis=0
        ).astype(BF16)
        kcols = slice(k * QDIM, (k + 1) * QDIM)
        vcols = slice((KVHEADS + k) * QDIM, (KVHEADS + k + 1) * QDIM)
        keys = jnp.concatenate([cache[:, :, kcols].reshape(KEYS, QDIM), extra[:, kcols]], axis=0)
        vals = jnp.concatenate([cache[:, :, vcols].reshape(KEYS, QDIM), extra[:, vcols]], axis=0)
        s = lax.dot_general(qk, keys, NT, preferred_element_type=F32) * SCALE
        s = jnp.where(valid, s.reshape(QPK, 8, KEYS + EXTRA), NEG)
        top = jnp.max(s, axis=2, keepdims=True)
        w = jnp.where(valid, jnp.exp(s - top), 0.0).astype(BF16)
        total = jnp.sum(w.astype(F32), axis=2, keepdims=True)
        acc = jnp.dot(w.reshape(QPK * 8, KEYS + EXTRA), vals, preferred_element_type=F32)
        some = total > 0.0
        safe = jnp.where(some, total, 1.0)
        lse = jnp.where(some, top + jnp.log(safe), NEG)
        o = acc.reshape(QPK, 8, QDIM) / safe
        out = jnp.where(sub == 6, stats_row(lse, sub, lane3), o)
        blocks[k] = out.reshape(QPK * 8, QDIM).astype(BF16)
        gone = sub == slot + 3
        scr[k * QPK : (k + 1) * QPK, :] = jnp.sum(jnp.where(gone, o, 0.0), axis=1)
        a, b, c = split3(jnp.sum(jnp.where(gone, lse, 0.0), axis=1))
        stats = jnp.where(lane2 == 3 * k, a, stats)
        stats = jnp.where(lane2 == 3 * k + 1, b, stats)
        stats = jnp.where(lane2 == 3 * k + 2, c, stats)
    scr[LSE : LSE + QPK, :] = stats
    leaving[:MOVED, :] = scr[...].astype(BF16)


def partials(lens, table, mig, swapped, *rest):
    return call(
        partial_body,
        (
            like(KVHEADS + 1, QPK * 8, QDIM),
            like(MOVED + STATE_ROWS, 128),
        ),
        scalars(2) + [whole(mig)] + here(1) + [whole(a) for a in rest],
        tuple(here(2)),
        [
            VMEM((8, QHEADS * QDIM), F32),
            VMEM((EXTRA, KVW), F32),
            VMEM((8, COLS), F32),
            VMEM((8, COLS), F32),
            VMEM((8, 128), F32),
            VMEM((8, STATE), F32),
            VMEM((8, STATE), F32),
            VMEM((MOVED, 128), F32),
        ],
        name="partials",
    )(lens, table, mig, swapped, *rest)


def insert_body(mig, blocks, moved, out, gated_out):
    slot = slot_of(mig)
    sub = iota((QPK, 8, 128), 1)
    lane = iota((QPK, 8, 128), 2)
    mv = moved[:MOVED, :].astype(F32)
    g = flat(mv[GHI : GHI + 4] + mv[GLO : GLO + 4])
    g = jnp.where(iota((8, COLS), 0) == slot + 3, g, unpack_rows(blocks[KVHEADS]))
    gated_out[...] = g
    squares = jnp.sum(g * g, axis=1, keepdims=True)
    sq_row = stats_row(squares[None], sub[:1], lane[:1])
    stats = mv[LSE : LSE + QPK]
    lane2 = iota((QPK, 128), 1)
    mine = jnp.logical_and(lane < 24, lane % 8 == slot + 3)
    for k in range(KVHEADS):
        lse = jnp.where(lane2 // 3 == k, stats, 0.0)
        lse = jnp.sum(lse, axis=1, keepdims=True)[:, None, :]
        a, b, c = split3(jnp.broadcast_to(lse, (QPK, 8, 128)))
        terms = jnp.where(lane < 8, a, jnp.where(lane < 16, b, c))
        v = blocks[k].astype(F32).reshape(QPK, 8, 128)
        v = jnp.where(sub == slot + 3, mv[k * QPK : (k + 1) * QPK][:, None, :], v)
        v = jnp.where(jnp.logical_and(sub == 6, mine), terms, v)
        v = jnp.where(sub == 7, sq_row, v)
        v = v.reshape(QPK * 8, 128).astype(BF16)
        for z in range(2):
            out[k // 2 * 4 + z * 2 + k % 2] = v


def insert(mig, blocks, moved):
    return call(
        insert_body,
        (like(2 * KVHEADS, QPK * 8, QDIM), like(8, COLS, dtype=F32)),
        [whole(mig)] + here(2),
        tuple(here(2)),
        vmem=8,
        name="insert",
    )(mig, blocks, moved)


def finish_body(recv, gated, gain, blocks, m1, m2, scr):
    x = lax.axis_index("tp") // 4
    sub = iota((QPK, 8, 128), 1)
    lane = iota((QPK, 8, 128), 2)
    n = recv.shape[0]
    lses = [stats_col(recv[j].astype(F32).reshape(QPK, 8, 128)[:, 6:7], sub, lane) for j in range(n)]
    top = functools.reduce(jnp.maximum, lses)
    total = jnp.zeros_like(top)
    acc = jnp.zeros((QPK, 8, 128), F32)
    for j in range(n):
        w = jnp.exp(lses[j] - top)
        total += w
        acc += w * recv[j].astype(F32).reshape(QPK, 8, 128)
    o = (acc / total).reshape(QPK * 8, 128).astype(BF16)
    for k in range(KVHEADS):
        blocks[k] = o

    rows = recv[4 * x].astype(F32)[7:8]
    for j in range(1, 4):
        rows += recv[4 * x + j].astype(F32)[7:8]
    squares = stats_col(rows[None], sub[:1], lane[:1])[0]
    scr[...] = gated[...] * lax.rsqrt(squares * (1.0 / NORM) + 1e-05) * gain[...]
    m1[...] = scr[0:3, :].astype(BF16)
    m2[...] = scr[3:6, :].astype(BF16)


def finish(recv, gated, gain):
    return call(
        finish_body,
        (like(KVHEADS, QPK * 8, 128), like(REQ, COLS), like(REQ, COLS)),
        here(2) + [whole(gain)],
        tuple(here(3)),
        [VMEM((8, COLS), F32)],
        vmem=8,
        name="finish",
    )(recv, gated, gain)


def spread_body(recv, a1, a2, scr):
    for k in range(KVHEADS):
        rows = recv[k].astype(F32)
        for h in range(QPK):
            at = (k * QPK + h) * QDIM
            scr[:, at : at + QDIM] = rows[h * 8 : (h + 1) * 8]
    a1[...] = scr[0:3, :].astype(BF16)
    a2[...] = scr[3:6, :].astype(BF16)


def spread(recv):
    n = QHEADS * QDIM
    return call(
        spread_body,
        (like(REQ, n),) * 2,
        here(1),
        tuple(here(2)),
        [VMEM((8, n), F32)],
        vmem=8,
        name="spread",
    )(recv)


def update_body(mig, swapped, moved, x1, dt1, b1, rate, bias, x2, dt2, b2, state, out, x8, d8, b8):
    slot = slot_of(mig)
    r = pl.program_id(0)
    cols = group_cols()
    sw = swapped[:SWAP, :].astype(F32)

    def rows8(scr, one, two, moved):
        n = one.shape[-1]
        scr[...] = jnp.zeros_like(scr)
        scr[0:3, :n] = jnp.where(iota((3, n), 0) == slot, moved, one.astype(F32))
        scr[3:6, :n] = two.astype(F32)
        return scr[...]

    xx = rows8(x8, x1[...], x2[...], flat(sw[X1 : X1 + 4]))
    bb = rows8(b8, b1[:, cols], b2[:, cols], flat(sw[B1 : B1 + 2]))
    dd = rows8(d8, dt1[...], dt2[...], sw[D1 : D1 + 1, :HEADS])
    dt = softplus(expand(dd, 8) + expand(bias[...], 1))
    decay = jnp.exp(-dt * expand(rate[...], 1))
    pushed = dt * xx
    later = pltpu.roll(decay, 5, 0)
    row = iota((8, COLS), 0)
    u = jnp.where(row < 3, pushed * later, pushed)
    both = jnp.sum(jnp.where(row == r, decay * later, 0.0), axis=0, keepdims=True)
    mine = jnp.logical_or(row == r, row == r + 3)
    bh = bb.astype(BF16)
    add = jnp.zeros((COLS, STATE), F32)
    for part in hi_lo(jnp.where(mine, u, 0.0)):
        add += lax.dot_general(part, bh, (((0,), (0,)), ((), ())), preferred_element_type=F32)
    new = r == slot
    for h in range(HEADS):
        if h < HALF:
            arrived = load_state(swapped, SWAP, h)
        else:
            arrived = load_state(moved, MOVED, h - HALF)
        s = jnp.where(new, arrived.astype(F32), state[0, h])
        d = both[:, h * HDIM : h * HDIM + 1]
        out[0, h] = d * s + add[h * HDIM : (h + 1) * HDIM]


def update(mig, swapped, moved, *rest):
    state = rest[-1]
    block = pl.BlockSpec((1,) + state.shape[1:], lambda r: (r, 0, 0, 0))
    return call(
        update_body,
        like(*state.shape, dtype=F32),
        [whole(mig)] + here(2) + [whole(a) for a in rest[:-1]] + [block],
        block,
        [VMEM((8, COLS), F32), VMEM((8, 128), F32), VMEM((8, STATE), F32)],
        grid=(REQ,),
        name="update",
    )(mig, swapped, moved, *rest)


PLANE = [[x * 4 + z * 2 + c for x in range(4) for c in range(2)] for z in range(2)]


def swap(m, v):
    return lax.ppermute(v, "inst", [(s, s ^ m) for s in range(lax.axis_size("inst"))])


def shards(
    x_one, z_one, dt_one, b_one, c_one, q_one, kv_one, state, cache, page_table,
    lengths, migration, decay_rate, dt_bias, skip_gain, norm_gain,
    x_two, z_two, dt_two, b_two, c_two, q_two, kv_two,
):
    rate, bias, skip, gain = decay_rate[None], dt_bias[None], skip_gain[None], norm_gain[None]
    migration = migration.T

    def by_partner(body, *operands):
        ways = range(1, lax.axis_size("inst"))
        return lax.switch(pairing - 1, [functools.partial(body, m) for m in ways], *operands)

    payload, pairing = prepare(
        migration, x_one, dt_one, b_one, q_two, kv_two, x_two, z_two, dt_two, b_two, c_two, state
    )
    pairing = pairing[0]
    swapped = by_partner(swap, payload)
    blocks, leaving = partials(
        lengths, page_table, migration, swapped,
        x_one, z_one, dt_one, b_one, c_one, q_one, kv_one, state, cache,
        rate, bias, skip, x_two, z_two, dt_two, b_two, c_two, q_two, kv_two,
    )
    moved = by_partner(swap, leaving)
    blocks, gated = insert(migration, blocks, moved)
    recv = lax.all_to_all(blocks, "tp", 0, 0)
    blocks, mamba_one, mamba_two = finish(recv, gated, gain)
    recv = lax.all_to_all(blocks, "tp", 0, 0, axis_index_groups=PLANE)
    attn_one, attn_two = spread(recv)
    state_out = update(
        migration, swapped, moved, x_one, dt_one, b_one, rate, bias, x_two, dt_two, b_two, state
    )
    return mamba_one, attn_one, mamba_two, attn_two, state_out


def solution(mesh):
    row = P("inst", "tp")
    wide = P("inst", None)
    head = P("tp")
    states = P("inst", "tp", None, None)
    return jax.shard_map(
        shards,
        mesh=mesh,
        in_specs=(
            row, row, row, wide, wide, wide, wide, states, P("inst", None, "tp"), row,
            P(), P(), head, head, head, head, row, row, row, wide, wide, wide, wide,
        ),
        out_specs=(row, wide, row, wide, states),
        check_vma=False,
    )
```
